128 devices in a mesh: ctx: 32 (over z_lo, y, x), head: 4 (over z_hi, core).
Axes of the slice: x: 4, y: 4, z: 4 (z_hi: 2, z_lo: 2; z = z_hi * 2 + z_lo), core: 2. Of those that a mesh axis runs over, the one named last changes fastest.
Arguments:
- query: bfloat16 [8192, 4096], P('ctx', 'head'), may hold values from -3 to 3
- key: bfloat16 [8192, 512], P('ctx', 'head'), may hold values from -3 to 3
- value: bfloat16 [8192, 512], P('ctx', 'head'), may hold values from -6 to 6
- attention_out: bfloat16 [8192, 4096], P('ctx', 'head'), may hold values from -6 to 6
- out_grad: bfloat16 [8192, 4096], P('ctx', 'head'), may hold values from -6 to 6
- log_norm: float32 [8192, 32], P('ctx', 'head'), may hold values from 0 to 12
- span_order: int32 [64], P('ctx'), may hold values from 0 to 63, as said below
- span_segment: int32 [64], P('ctx'), may hold values from 0 to 63, as said below
- key_weight: bfloat16 [8192, 512], P(None, 'head'), may hold values from -0.0625 to 0.0625
- value_weight: bfloat16 [8192, 512], P(None, 'head'), may hold values from -0.0625 to 0.0625
Outputs:
- query_grad: bfloat16 [8192, 4096], P('ctx', 'head')
- key_grad: bfloat16 [8192, 512], P('ctx', 'head')
- value_grad: bfloat16 [8192, 512], P('ctx', 'head')
- input_grad: bfloat16 [8192, 8192], P('ctx', 'head')
The draws below stay inside these ranges and needn't reach their ends.
Inputs may be any that keep to these rules, and one draw needn't show every extreme that they name: `span_order`: each device's two slots hold spans c and 63 - c; every span lies in exactly one slot. `span_segment`: documents are runs of whole spans, each named by the index in the sequence of its first span; the last span of the sequence is a document of its own.
All inputs are finite; a program needn't handle non-finite values.
Results may differ from the reference program's by a relative error of at most 0.018.
Values may be sent and summed in bfloat16 or wider, within the bound.
A program may use at most 64 MiB of HBM per device.

```python
import math
import jax
import jax.numpy as jnp
from jax import lax

D = 8192
HEAD_DIM = 128
GROUP = 8
KV_HEADS = 4
SPAN = 128
SPANS = 64
TOKENS = 8192
Q_HEADS = 32


def layout_tables(key):
    half = SPANS // 2
    shuffle = jax.random.permutation(key, half).astype(jnp.int32)
    order = jnp.stack([shuffle, SPANS - 1 - shuffle], axis=1).reshape(SPANS).astype(jnp.int32)
    marks = jax.random.randint(jax.random.fold_in(key, 11), (SPANS,), 0, 32)
    places = jnp.arange(SPANS, dtype=jnp.int32)
    opening = (marks == 0) | (places == 0) | (places == SPANS - 1)
    first_span = lax.cummax(jnp.where(opening, places, 0), axis=0).astype(jnp.int32)
    return (order, first_span[order].astype(jnp.int32), first_span)


def draw_span_order(key, part):
    tables = layout_tables(key)
    return tables[0]


def draw_span_segment(key, part):
    tables = layout_tables(key)
    return tables[1]


def draw_log_norm(key, part):
    order, stored, first_span = layout_tables(key)
    key = jax.random.fold_in(key, 3)
    rows = jnp.arange(TOKENS, dtype=jnp.int32)
    true_span = order[rows // SPAN]
    place = true_span * SPAN + rows % SPAN
    visible_count = place - first_span[true_span] * SPAN + 1
    log_count = jnp.log(visible_count.astype(jnp.float32))
    offset = jax.random.uniform(key, (TOKENS, Q_HEADS), jnp.float32, 0.2, 0.8)
    return (log_count[:, None] + offset).astype(jnp.float32)


def bounded_field(key, shape):
    field = jnp.clip(jax.random.normal(key, shape, jnp.float32), -3.0, 3.0)
    return field


def draw_query(key, part):
    key = jax.random.fold_in(key, 5)
    return bounded_field(key, (TOKENS, Q_HEADS * HEAD_DIM)).astype(jnp.bfloat16)


def draw_key(key, part):
    key = jax.random.fold_in(key, 7)
    return bounded_field(key, (TOKENS, KV_HEADS * HEAD_DIM)).astype(jnp.bfloat16)


def block_scale(own_key, shape, shards, low, largest):
    loudness = 1.0
    for dim, blocks in shards:
        steps = jax.random.uniform(jax.random.fold_in(jax.random.fold_in(own_key, 6), dim), (blocks,), jnp.float32, low / len(shards), largest / len(shards))
        loudness = loudness * jnp.repeat(jnp.exp(steps), shape[dim] // blocks).reshape((-1,) + (1,) * (len(shape) - 1 - dim))
    return loudness


def normal_values(rng, dims, spread, limit, cuts=(), kind=jnp.bfloat16):
    values = spread * jax.random.normal(rng, dims, jnp.float32)
    if cuts:
        values = values * block_scale(rng, dims, cuts, -0.22, 0.18)
    return jnp.clip(values, -limit, limit).astype(kind)


def setup_inputs(seed: int = 0) -> dict:
    key_list = jax.random.split(jax.random.key(seed), 11)
    query = draw_query(jax.random.fold_in(key_list[10], 71), 0)
    key = draw_key(jax.random.fold_in(key_list[10], 71), 0)
    value = normal_values(key_list[2], (TOKENS, KV_HEADS * HEAD_DIM), 1.0, 6.0, ((0, 32), (1, 4)))
    attention_out = normal_values(key_list[3], (TOKENS, Q_HEADS * HEAD_DIM), 1.0, 6.0, ((0, 32), (1, 4)))
    out_grad = normal_values(key_list[4], (TOKENS, Q_HEADS * HEAD_DIM), 1.0, 6.0, ((0, 32), (1, 4)))
    log_norm = draw_log_norm(jax.random.fold_in(key_list[10], 71), 0)
    span_order = draw_span_order(jax.random.fold_in(key_list[10], 71), 0)
    span_segment = draw_span_segment(jax.random.fold_in(key_list[10], 71), 0)
    key_weight = normal_values(key_list[8], (D, KV_HEADS * HEAD_DIM), D ** -0.5, 0.0625, ((1, 4),))
    value_weight = normal_values(key_list[9], (D, KV_HEADS * HEAD_DIM), D ** -0.5, 0.0625, ((1, 4),))
    return {"query": query, "key": key, "value": value, "attention_out": attention_out, "out_grad": out_grad, "log_norm": log_norm, "span_order": span_order, "span_segment": span_segment, "key_weight": key_weight, "value_weight": value_weight}


def row_tables(span_order, span_segment):
    rows = jnp.arange(TOKENS, dtype=jnp.int32)
    slot = rows // SPAN
    position = span_order[slot] * SPAN + rows % SPAN
    document = span_segment[slot]
    return (position.astype(jnp.int32), document.astype(jnp.int32))

def rounded(values):
    low = values.astype(jnp.bfloat16)
    low = lax.optimization_barrier(low)
    return low.astype(jnp.float32)

def reference(query, key, value, attention_out, out_grad, log_norm, span_order, span_segment, key_weight, value_weight):
    scale = 1.0 / math.sqrt(HEAD_DIM)
    position, document = row_tables(span_order, span_segment)
    queries = query.astype(jnp.float32).reshape(TOKENS, KV_HEADS, GROUP, HEAD_DIM)
    grads = out_grad.astype(jnp.float32).reshape(TOKENS, KV_HEADS, GROUP, HEAD_DIM)
    outputs = attention_out.astype(jnp.float32).reshape(TOKENS, KV_HEADS, GROUP, HEAD_DIM)
    delta = lax.optimization_barrier(jnp.sum(grads * outputs, axis=-1))
    norms = log_norm.astype(jnp.float32).reshape(TOKENS, KV_HEADS, GROUP)
    keys = key.astype(jnp.float32).reshape(TOKENS, KV_HEADS, HEAD_DIM)
    values = value.astype(jnp.float32).reshape(TOKENS, KV_HEADS, HEAD_DIM)
    block = math.gcd(512, TOKENS)
    count = TOKENS // block
    query_parts = []
    key_parts = []
    value_parts = []
    for head in range(KV_HEADS):
        head_keys = keys[:, head]
        head_values = values[:, head]
        head_queries = queries[:, head]
        head_grads = grads[:, head]
        head_norms = norms[:, head]
        head_delta = delta[:, head]

        def step(carry, index):
            key_acc, value_acc = carry
            start = index * block
            block_query = lax.dynamic_slice_in_dim(head_queries, start, block, 0)
            block_grad = lax.dynamic_slice_in_dim(head_grads, start, block, 0)
            block_norm = lax.dynamic_slice_in_dim(head_norms, start, block, 0)
            block_delta = lax.dynamic_slice_in_dim(head_delta, start, block, 0)
            block_position = lax.dynamic_slice_in_dim(position, start, block, 0)
            block_document = lax.dynamic_slice_in_dim(document, start, block, 0)
            visible = (block_document[:, None] == document[None, :]) & (position[None, :] <= block_position[:, None])
            scores = jnp.einsum('igd,jd->gij', block_query, head_keys) * scale
            attend = jnp.where(visible[None], jnp.exp(scores - jnp.transpose(block_norm)[:, :, None]), 0.0)
            attend_low = rounded(attend)
            attend_grad = jnp.einsum('igd,jd->gij', block_grad, head_values)
            score_grad = attend * (attend_grad - jnp.transpose(block_delta)[:, :, None])
            score_low = rounded(score_grad)
            value_acc = value_acc + jnp.einsum('gij,igd->jd', attend_low, block_grad)
            key_acc = key_acc + jnp.einsum('gij,igd->jd', score_low, block_query) * scale
            query_block = jnp.einsum('gij,jd->igd', score_low, head_keys) * scale
            return ((key_acc, value_acc), query_block)
        zeros = jnp.zeros((TOKENS, HEAD_DIM), jnp.float32)
        (key_acc, value_acc), blocks = lax.scan(step, (zeros, zeros), jnp.arange(count, dtype=jnp.int32))
        query_parts.append(blocks.reshape(TOKENS, GROUP * HEAD_DIM))
        key_parts.append(key_acc)
        value_parts.append(value_acc)
    query_grad = jnp.concatenate(query_parts, axis=1).astype(jnp.bfloat16)
    key_grad = jnp.concatenate(key_parts, axis=1).astype(jnp.bfloat16)
    value_grad = jnp.concatenate(value_parts, axis=1).astype(jnp.bfloat16)
    input_grad = jnp.dot(key_grad, key_weight.T, preferred_element_type=jnp.float32)
    input_grad = input_grad + jnp.dot(value_grad, value_weight.T, preferred_element_type=jnp.float32)
    return (query_grad, key_grad, value_grad, input_grad.astype(jnp.bfloat16))
```

```python
import math

import jax
import jax.numpy as jnp
from jax import lax
from jax.experimental import pallas as pl
from jax.experimental.pallas import tpu as pltpu
from jax.sharding import PartitionSpec as P

HEAD_DIM = 128
SPAN = 128
GROUP = 8
SCALE = 1.0 / math.sqrt(HEAD_DIM)
LOG2E = math.log2(math.e)
HIDDEN = -1e30
MESH = pl.DeviceIdType.MESH
F32, BF16, I32 = jnp.float32, jnp.bfloat16, jnp.int32
NN = (((1,), (0,)), ((), ()))
NT = (((1,), (1,)), ((), ()))
PIECE = 4 * SPAN
STEPS = 5
ENTRIES = 4 * STEPS
EMPTY, DIAG_HI, DIAG_LO = ENTRIES, ENTRIES + 1, ENTRIES + 2
AROUND = (1, 3, 2)


def dot(a, b, dims=NN):
    return lax.dot_general(a, b, dims, preferred_element_type=F32)


def kernel(q, do, o, norm, k, v, order, segment, wk, wv, dq_out, dk_out, dv_out, ig_out, *scratch):
    names = [n for n, _ in SCRATCH]
    s = dict(zip(names, scratch))
    qs, ds = [s[f"qs{i}"] for i in range(4)], [s[f"ds{i}"] for i in range(4)]
    qt, dt = [s[f"qt{i}"] for i in range(4)], [s[f"dt{i}"] for i in range(4)]
    nrm, dlt = [s[f"nrm{i}"] for i in range(4)], [s[f"dlt{i}"] for i in range(4)]
    dqa = [s[f"dqa{i}"] for i in range(4)]
    nd = [s["nd0"], s["nd1"]]
    tab, tabz = s["tab"], s["tabz"]
    kbuf, vbuf, acck, accv = s["kbuf"], s["vbuf"], s["acck"], s["accv"]
    bk, bv = [s["bk0"], s["bk1"]], [s["bv0"], s["bv1"]]
    pos_lo, pos_hi, ent, vis, turn = s["pos_lo"], s["pos_hi"], s["ent"], s["vis"], s["turn"]
    kg, wg = s["kg"], s["wg"]

    ctx, head = lax.axis_index("ctx"), lax.axis_index("head")
    z, y, x = ctx // 16, (ctx // 4) % 4, ctx % 4
    me = y * 4 + x

    def at_x(d):
        return (z * 16 + y * 4 + (x + d) % 4, head)

    def at_y(d):
        return (z * 16 + ((y + d) % 4) * 4 + x, head)

    over = ((1 - z) * 16 + me, head)
    mate = head + 1 - 2 * (head % 2)
    far, far_mate = (head + 2) % 4, 3 - head
    weight_peers = ((ctx, mate), ((1 - z) * 16 + me, far), ((1 - z) * 16 + me, far_mate))
    head_peers = ((ctx, mate), (ctx, far), (ctx, far_mate))

    barrier = pltpu.get_barrier_semaphore()
    peers = [at_x(d) for d in AROUND] + [at_y(d) for d in AROUND] + [over]
    peers += [weight_peers[0], weight_peers[1], weight_peers[2], head_peers[1], head_peers[2]]
    for peer in peers:
        pl.semaphore_signal(barrier, inc=1, device_id=peer, device_id_type=MESH)

    sent = []

    def copy(src, dst, send, recv, peer):
        return pltpu.make_async_remote_copy(
            src_ref=src, dst_ref=dst, send_sem=send, recv_sem=recv, device_id=peer, device_id_type=MESH
        )

    def push(src, dst, send, recv, peer):
        c = copy(src, dst, send, recv, peer)
        c.start()
        sent.append(c)

    def arrived(dst, send, recv):
        copy(dst, dst, send, recv, over).wait_recv()

    def swapped(sel, first, second):
        shape = first.shape
        turn_round = jnp.full(shape, order[0], I32) > jnp.full(shape, order[1], I32)
        return jnp.where(turn_round, second, first) if sel == 0 else jnp.where(turn_round, first, second)

    slots = (pl.ds(0, SPAN), pl.ds(SPAN, SPAN))

    for sel in range(2):
        kbuf[2 * me + sel] = swapped(sel, k[slots[0], :], k[slots[1], :])
        vbuf[2 * me + sel] = swapped(sel, v[slots[0], :], v[slots[1], :])
    for i, value in enumerate((order[0], order[1], segment[0], segment[1])):
        tab[me, 0, i] = value

    def stack(p):
        for sel in range(2):
            for hh in range(4):
                r = pl.ds(hh * SPAN, SPAN)
                c = pl.ds((p * 4 + hh) * HEAD_DIM, HEAD_DIM)
                qs[p][sel, r, :] = swapped(sel, q[slots[0], c], q[slots[1], c])
                ds[p][sel, r, :] = swapped(sel, do[slots[0], c], do[slots[1], c])

    stack(0)
    stack(1)
    pl.semaphore_wait(barrier, len(peers))

    ks, vs = s["k_send"], s["v_send"]
    kr, vr = s["k_recv"], s["v_recv"]
    own = pl.ds(2 * me, 2)
    ms, mr, mrow = s["m_send"], s["m_recv"], s["m_row"]
    for i, d in enumerate(AROUND):
        push(tab.at[me], tab.at[me], ms.at[i], mr.at[me], at_x(d))
    for i, d in enumerate(AROUND):
        push(kbuf.at[own], kbuf.at[own], ks.at[i], kr.at[me], at_x(d))
        push(vbuf.at[own], vbuf.at[own], vs.at[i], vr.at[me], at_y(d))
    zs, zr = s["z_send"], s["z_recv"]
    push(tab.at[me], tabz.at[0], ms.at[6], s["mz_recv"].at[0], over)
    push(qs[0], qs[2], zs.at[0], zr.at[0], over)
    push(ds[0], ds[2], zs.at[1], zr.at[1], over)
    for i, d in enumerate(AROUND):
        push(kbuf.at[own], kbuf.at[own], ks.at[3 + i], kr.at[me], at_y(d))
        push(vbuf.at[own], vbuf.at[own], vs.at[3 + i], vr.at[me], at_x(d))
    ws, wr = s["w_send"], s["w_recv"]
    fill = []
    for i, w in enumerate((wk, wv)):
        columns = w.shape[0] // 4
        for j, peer in enumerate(weight_peers):
            rows = pl.ds(pl.multiple_of(peer[1] * columns, columns), columns)
            push(w.at[rows], wg.at[i, head], ws.at[3 * i + j], wr.at[4 * i + head], peer)
        rows = pl.ds(pl.multiple_of(head * columns, columns), columns)
        fill.append(pltpu.make_async_copy(w.at[rows], wg.at[i, head], s["fill"].at[i]))
        fill[-1].start()

    lane = lax.broadcasted_iota(I32, (2 * SPAN, 128), 1)
    sums = jnp.zeros((2 * SPAN, 128), F32)
    for h in range(GROUP):
        c = pl.ds(h * HEAD_DIM, HEAD_DIM)
        term = jnp.sum(do[:, c].astype(F32) * o[:, c].astype(F32), axis=1, keepdims=True)
        sums = jnp.where(lane == h, term, sums)
    sums = sums.T[0:8, :]
    for sel in range(2):
        c = pl.ds(sel * SPAN, SPAN)
        nd[0][0:8, c] = swapped(sel, norm[:, slots[0]], norm[:, slots[1]])
        nd[0][8:16, c] = swapped(sel, sums[:, :SPAN], sums[:, SPAN:])
    push(nd[0], nd[1], zs.at[2], zr.at[2], over)
    push(qs[1], qs[3], zs.at[3], zr.at[3], over)
    push(ds[1], ds[3], zs.at[4], zr.at[4], over)

    def spread(g):
        rows = jnp.concatenate([nd[g][...], jnp.zeros((112, 2 * SPAN), F32)], axis=0).T
        for p in range(2):
            for sel in range(2):
                part = rows[sel * SPAN : (sel + 1) * SPAN, :]
                for hh in range(4):
                    h, r = p * 4 + hh, pl.ds(hh * SPAN, SPAN)
                    nrm[2 * g + p][sel, r, :] = jnp.broadcast_to(part[:, h : h + 1] * LOG2E, (SPAN, 128))
                    dlt[2 * g + p][sel, r, :] = jnp.broadcast_to(part[:, 8 + h : 9 + h], (SPAN, 128))

    def turned(i):
        for sel in range(2):
            for hh in range(4):
                r = pl.ds(hh * SPAN, SPAN)
                qt[i][sel, :, r] = qs[i][sel, r, :].T
                dt[i][sel, :, r] = ds[i][sel, r, :].T

    def step(i, sel, k4, v4, bias=None, mask=None):
        n = k4.shape[0] // 128
        e = dot(qs[i][sel], k4, NT) * (SCALE * LOG2E) - jnp.concatenate([nrm[i][sel]] * n, axis=1)
        if bias is not None:
            e = e + bias
        if mask is not None:
            e = jnp.where(mask, e, HIDDEN)
        attend = jnp.exp2(e)
        grad = dot(ds[i][sel], v4, NT) - jnp.concatenate([dlt[i][sel]] * n, axis=1)
        score = (attend * grad).astype(BF16)
        return score, dot(qt[i][sel], score), dot(dt[i][sel], attend.astype(BF16))

    def bias_row(seen):
        return jnp.concatenate(
            [jnp.where(jnp.full((1, 128), one, I32) > 0, 0.0, HIDDEN) for one in seen], axis=1
        )

    def columns_of(a, u):
        return a[:, u * 128 : (u + 1) * 128]

    spread(0)
    turned(0)
    turned(1)
    row = lax.broadcasted_iota(I32, (PIECE, 128), 0) % SPAN
    below = lax.broadcasted_iota(I32, (PIECE, 128), 1) <= row
    for sel in range(2):
        k1, v1 = kbuf[2 * me + sel], vbuf[2 * me + sel]
        place = DIAG_HI if sel else DIAG_LO
        score, dk0, dv0 = step(0, sel, k1, v1, mask=below)
        dqa[0][sel] = dot(score, k1)
        score, dk1, dv1 = step(1, sel, k1, v1, mask=below)
        dqa[1][sel] = dot(score, k1)
        bk[0][place] = dk0 + dk1
        bv[0][place] = dv0 + dv1
    for g in range(2):
        bk[g][EMPTY] = jnp.zeros((128, 128), F32)
        bv[g][EMPTY] = jnp.zeros((128, 128), F32)
    for i in (2, 3):
        dqa[i][...] = jnp.zeros_like(dqa[i])

    for i, d in enumerate(AROUND):
        arrived(tab.at[y * 4 + (x + 4 - d) % 4], ms.at[0], mr.at[y * 4 + (x + 4 - d) % 4])
    for i, d in enumerate(AROUND):
        line = pl.ds(y * 4, 4)
        push(tab.at[line], tab.at[line], ms.at[3 + i], mrow.at[y], at_y(d))
    for i, d in enumerate(AROUND):
        j = y * 4 + (x + 4 - d) % 4
        two = pl.ds(2 * j, 2)
        arrived(kbuf.at[two], ks.at[0], kr.at[j])
        for n, e in enumerate(AROUND):
            push(kbuf.at[two], kbuf.at[two], ks.at[6 + 3 * i + n], kr.at[j], at_y(e))
        j = ((y + 4 - d) % 4) * 4 + x
        two = pl.ds(2 * j, 2)
        arrived(vbuf.at[two], vs.at[0], vr.at[j])
        for n, e in enumerate(AROUND):
            push(vbuf.at[two], vbuf.at[two], vs.at[6 + 3 * i + n], vr.at[j], at_x(e))

    def low_span(j):
        return jnp.minimum(tab[j, 0, 0], tab[j, 0, 1])

    def query_spans(t, j):
        first = t[j, 0, 0] < t[j, 0, 1]
        low = jnp.where(first, t[j, 0, 0], t[j, 0, 1])
        return low, jnp.where(first, t[j, 0, 2], t[j, 0, 3]), jnp.where(first, t[j, 0, 3], t[j, 0, 2])

    def later_rows(pieces, r, seg_hi, fresh):
        j0 = ((y + r) % 4) * 4
        k4 = jnp.concatenate([kbuf[2 * (j0 + u)] for u in range(4)], axis=0)
        v4 = jnp.concatenate([vbuf[2 * (j0 + u)] for u in range(4)], axis=0)
        bias = bias_row([low_span(j0 + u) - seg_hi + 1 for u in range(4)])
        dks = dvs = None
        for i in pieces:
            score, dk, dv = step(i, 1, k4, v4, bias=bias)
            dqa[i][1] += dot(score, k4)
            dks, dvs = (dk, dv) if dks is None else (dks + dk, dvs + dv)
        for u in range(4):
            if fresh:
                acck[j0 + u] = columns_of(dks, u)
                accv[j0 + u] = columns_of(dvs, u)
            else:
                acck[j0 + u] += columns_of(dks, u)
                accv[j0 + u] += columns_of(dvs, u)

    def sorted_rows(pieces, g, t, fresh):
        sel = jnp.where(t >= turn[g], 1, 0)
        k4 = jnp.concatenate([kbuf[ent[g * ENTRIES + 4 * t + u]] for u in range(4)], axis=0)
        v4 = jnp.concatenate([vbuf[ent[g * ENTRIES + 4 * t + u]] for u in range(4)], axis=0)
        bias = bias_row([vis[g * ENTRIES + 4 * t + u] for u in range(4)])
        none = jnp.zeros_like(k4)
        early = jnp.full(k4.shape, sel, I32) == 0
        wide = jnp.concatenate([jnp.where(early, k4, none), jnp.where(early, none, k4)], axis=1)
        dks = dvs = None
        for i in pieces:
            score, dk, dv = step(i, sel, k4, v4, bias=bias)
            both = dot(score, wide)
            dqa[i][0] += both[:, :128]
            dqa[i][1] += both[:, 128:]
            dks, dvs = (dk, dv) if dks is None else (dks + dk, dvs + dv)
        for u in range(4):
            if fresh:
                bk[g][4 * t + u] = columns_of(dks, u)
                bv[g][4 * t + u] = columns_of(dvs, u)
            else:
                bk[g][4 * t + u] += columns_of(dks, u)
                bv[g][4 * t + u] += columns_of(dvs, u)

    lo_own, seg_lo_own, seg_hi_own = query_spans(tab, me)

    def own_line(r, _):
        j0 = ((y + r) % 4) * 4
        for u in range(4):
            j = j0 + u
            two = pl.ds(2 * j, 2)

            @pl.when(r > 0)
            def _():
                arrived(kbuf.at[two], ks.at[0], kr.at[j])

            @pl.when(x != u)
            def _():
                arrived(vbuf.at[two], vs.at[0], vr.at[j])

        @pl.when(r > 0)
        def _():
            arrived(tab.at[pl.ds(j0, 4)], ms.at[0], mrow.at[(y + r) % 4])

        later_rows((0, 1), r, seg_hi_own, True)
        return 0

    lax.fori_loop(0, 4, own_line, 0)

    arrived(tabz.at[0], ms.at[0], s["mz_recv"].at[0])
    lo_over, seg_lo_over, seg_hi_over = query_spans(tabz, 0)
    for g, (low, seg_lo, seg_hi) in enumerate(
        ((lo_own, seg_lo_own, seg_hi_own), (lo_over, seg_lo_over, seg_hi_over))
    ):
        spans = [low_span(j) for j in range(16)]
        before = sum(jnp.where(one < low, 1, 0) for one in spans)
        upto = sum(jnp.where(one <= low, 1, 0) for one in spans)
        first = (before + 3) // 4
        turn[g] = first

        def place(j, _, g=g, low=low, spans=spans, upto=upto, first=first):
            mine = low_span(j)
            rank = sum(jnp.where(one < mine, 1, 0) for one in spans)
            hi = 4 * first + rank - upto
            pos_lo[16 * g + j] = jnp.where(mine < low, rank, jnp.where(mine == low, DIAG_LO, EMPTY))
            pos_hi[16 * g + j] = jnp.where(mine > low, hi, jnp.where(mine == low, DIAG_HI, EMPTY))
            return 0

        lax.fori_loop(0, 16, place, 0)

        def entry(p, _, g=g, spans=spans, first=first, seg_lo=seg_lo, seg_hi=seg_hi):
            index, span = jnp.int32(0), jnp.int32(-1)
            for j in range(16):
                is_lo, is_hi = pos_lo[16 * g + j] == p, pos_hi[16 * g + j] == p
                index = jnp.where(is_lo, 2 * j, jnp.where(is_hi, 2 * j + 1, index))
                span = jnp.where(is_lo, spans[j], jnp.where(is_hi, 63 - spans[j], span))
            seg = jnp.where(p < 4 * first, seg_lo, seg_hi)
            ent[g * ENTRIES + p] = index
            vis[g * ENTRIES + p] = jnp.where(span >= seg, 1, 0)
            return 0

        lax.fori_loop(0, ENTRIES, entry, 0)

    def own_sorted(t, _):
        sorted_rows((0, 1), 0, t, True)
        return 0

    lax.fori_loop(0, STEPS, own_sorted, 0)

    dqs, dqr = [s["dqs0"], s["dqs1"]], [s["dqr0"], s["dqr1"]]
    arrived(nd[1], zs.at[0], zr.at[2])
    spread(1)
    for p in range(2):
        i = 2 + p
        arrived(qs[i], zs.at[0], zr.at[3 * p])
        arrived(ds[i], zs.at[0], zr.at[3 * p + 1])
        turned(i)

        def over_line(r, _, i=i):
            later_rows((i,), r, seg_hi_over, False)
            return 0

        lax.fori_loop(0, 4, over_line, 0)

        def over_sorted(t, _, i=i, p=p):
            sorted_rows((i,), 1, t, p == 0)
            return 0

        lax.fori_loop(0, STEPS, over_sorted, 0)
        dqs[p][...] = dqa[i][...].astype(BF16)
        push(dqs[p], dqr[p], zs.at[5 + p], zr.at[5 + p], over)

    def total(acc, b, j):
        lo = acc[j] + b[0][pos_lo[j]] + b[1][pos_lo[16 + j]]
        hi = b[0][pos_hi[j]] + b[1][pos_hi[16 + j]]
        return jnp.concatenate([lo, hi], axis=1)

    sk, sv, r1k, r1v = s["sk"], s["sv"], s["r1k"], s["r1v"]
    for i, d in enumerate(AROUND):
        yd, xd = (y + d) % 4, (x + d) % 4

        def key_part(u, _, yd=yd):
            sk[yd * 4 + u] = total(acck, bk, yd * 4 + u).astype(BF16)
            return 0

        lax.fori_loop(0, 4, key_part, 0)
        push(sk.at[pl.ds(yd * 4, 4)], r1k.at[d - 1], s["s1"].at[i], s["s1r"].at[d - 1], at_y(d))

        def value_part(u, _, xd=xd):
            sv[xd * 4 + u] = total(accv, bv, u * 4 + xd).astype(BF16)
            return 0

        lax.fori_loop(0, 4, value_part, 0)
        push(sv.at[pl.ds(xd * 4, 4)], r1v.at[d - 1], s["s1"].at[3 + i], s["s1r"].at[2 + d], at_x(d))

    fk, fv, t2k, t2v, r2k, r2v = s["fk"], s["fv"], s["t2k"], s["t2v"], s["r2k"], s["r2v"]

    def own_part(u, _):
        fk[u] = total(acck, bk, y * 4 + u)
        fv[u] = total(accv, bv, u * 4 + x)
        return 0

    lax.fori_loop(0, 4, own_part, 0)
    for d in range(3):
        arrived(r1k.at[d], s["s1"].at[0], s["s1r"].at[d])

    def sum_keys(u, _):
        fk[u] += r1k[0, u].astype(F32) + r1k[1, u].astype(F32) + r1k[2, u].astype(F32)
        t2k[u] = fk[u].astype(BF16)
        return 0

    lax.fori_loop(0, 4, sum_keys, 0)
    for i, d in enumerate(AROUND):
        push(t2k.at[(x + d) % 4], r2k.at[d - 1], s["s2"].at[i], s["s2r"].at[d - 1], at_x(d))
    for d in range(3):
        arrived(r1v.at[d], s["s1"].at[0], s["s1r"].at[3 + d])

    def sum_values(u, _):
        fv[u] += r1v[0, u].astype(F32) + r1v[1, u].astype(F32) + r1v[2, u].astype(F32)
        t2v[u] = fv[u].astype(BF16)
        return 0

    lax.fori_loop(0, 4, sum_values, 0)
    for i, d in enumerate(AROUND):
        push(t2v.at[(y + d) % 4], r2v.at[d - 1], s["s2"].at[3 + i], s["s2r"].at[2 + d], at_y(d))

    for p in range(2):
        arrived(dqr[p], zs.at[0], zr.at[5 + p])
        for hh in range(4):
            r, c = pl.ds(hh * SPAN, SPAN), pl.ds((p * 4 + hh) * HEAD_DIM, HEAD_DIM)
            both = [(dqa[p][sel, r, :] + dqr[p][sel, r, :].astype(F32)) * SCALE for sel in range(2)]
            for slot in range(2):
                dq_out[slots[slot], c] = swapped(slot, both[0], both[1]).astype(BF16)

    for w, (f, r2, mine, out, scale) in enumerate(
        ((fk, r2k, x, dk_out, SCALE), (fv, r2v, y, dv_out, 1.0))
    ):
        for d in range(3):
            arrived(r2.at[d], s["s2"].at[0], s["s2r"].at[3 * w + d])
        whole = f[mine] + r2[0].astype(F32) + r2[1].astype(F32) + r2[2].astype(F32)
        both = [(columns_of(whole, sel) * scale).T for sel in range(2)]
        for slot in range(2):
            low = swapped(slot, both[0], both[1]).astype(BF16)
            out[slots[slot], :] = low
            kg[w, head, slots[slot], :] = low
        for i, peer in enumerate(head_peers):
            push(kg.at[w, head], kg.at[w, head], s["g_send"].at[3 * w + i], s["g_recv"].at[4 * w + head], peer)

    for w in range(2):
        fill[w].wait()
        for h in (mate, far, far_mate):
            arrived(wg.at[w, h], ws.at[0], wr.at[4 * w + h])
    for w in range(2):
        for h in (mate, far, far_mate):
            arrived(kg.at[w, h], ws.at[0], s["g_recv"].at[4 * w + h])

    def tile(n, _):
        cols = pl.ds(pl.multiple_of(n * 256, 256), 256)
        acc = None
        for w in range(2):
            for h in (0, 2):
                a = jnp.concatenate([kg[w, h], kg[w, h + 1]], axis=1)
                b = jnp.concatenate([wg[w, h, cols, :], wg[w, h + 1, cols, :]], axis=1)
                term = dot(a, b, NT)
                acc = term if acc is None else acc + term
        ig_out[:, cols] = acc.astype(BF16)
        return 0

    lax.fori_loop(0, ig_out.shape[1] // 256, tile, 0)
    for c in sent:
        c.wait_send()


def _scratch():
    v, dma, smem = pltpu.VMEM, pltpu.SemaphoreType.DMA, pltpu.SMEM
    out = []
    for i in range(4):
        out += [(f"qs{i}", v((2, PIECE, 128), BF16)), (f"ds{i}", v((2, PIECE, 128), BF16))]
        out += [(f"qt{i}", v((2, 128, PIECE), BF16)), (f"dt{i}", v((2, 128, PIECE), BF16))]
        out += [(f"nrm{i}", v((2, PIECE, 128), F32)), (f"dlt{i}", v((2, PIECE, 128), F32))]
        out += [(f"dqa{i}", v((2, PIECE, 128), F32))]
    for i in range(2):
        out += [(f"nd{i}", v((16, 256), F32)), (f"dqs{i}", v((2, PIECE, 128), BF16))]
        out += [(f"dqr{i}", v((2, PIECE, 128), BF16))]
        out += [(f"bk{i}", v((ENTRIES + 3, 128, 128), F32)), (f"bv{i}", v((ENTRIES + 3, 128, 128), F32))]
    out += [("tab", smem((16, 1, 128), I32)), ("tabz", smem((1, 1, 128), I32))]
    out += [("kbuf", v((32, 128, 128), BF16)), ("vbuf", v((32, 128, 128), BF16))]
    out += [("acck", v((16, 128, 128), F32)), ("accv", v((16, 128, 128), F32))]
    out += [("pos_lo", smem((32,), I32)), ("pos_hi", smem((32,), I32)), ("ent", smem((2 * ENTRIES,), I32))]
    out += [("vis", smem((2 * ENTRIES,), I32)), ("turn", smem((2,), I32))]
    out += [("sk", v((16, 128, 256), BF16)), ("sv", v((16, 128, 256), BF16))]
    for n in ("k", "v"):
        out += [(f"r1{n}", v((3, 4, 128, 256), BF16)), (f"f{n}", v((4, 128, 256), F32))]
        out += [(f"t2{n}", v((4, 128, 256), BF16)), (f"r2{n}", v((3, 128, 256), BF16))]
    out += [("kg", v((2, 4, 256, 128), BF16))]
    out += [("wg", v((2, 4, 2048, 128), BF16))]
    out += [("k_send", dma((15,))), ("v_send", dma((15,))), ("k_recv", dma((16,))), ("v_recv", dma((16,)))]
    out += [("m_send", dma((7,))), ("m_recv", dma((16,))), ("m_row", dma((4,))), ("mz_recv", dma((1,)))]
    out += [("z_send", dma((7,))), ("z_recv", dma((7,))), ("w_send", dma((6,))), ("w_recv", dma((8,)))]
    out += [("fill", dma((2,))), ("s1", dma((6,))), ("s1r", dma((6,))), ("s2", dma((6,))), ("s2r", dma((6,)))]
    out += [("g_send", dma((6,))), ("g_recv", dma((8,)))]
    return out


SCRATCH = _scratch()


def per_device(
    query, key, value, attention_out, out_grad, log_norm, span_order, span_segment, key_weight, value_weight
):
    rows = query.shape[0]
    vmem, smem = pl.BlockSpec(memory_space=pltpu.VMEM), pl.BlockSpec(memory_space=pltpu.SMEM)
    hbm = pl.BlockSpec(memory_space=pl.ANY)
    return pl.pallas_call(
        kernel,
        name="attention_backward",
        out_shape=(
            jax.ShapeDtypeStruct(query.shape, BF16),
            jax.ShapeDtypeStruct(key.shape, BF16),
            jax.ShapeDtypeStruct(value.shape, BF16),
            jax.ShapeDtypeStruct((rows, key_weight.shape[0] // 4), BF16),
        ),
        in_specs=[vmem] * 6 + [smem] * 2 + [hbm] * 2,
        out_specs=(vmem,) * 4,
        scratch_shapes=[shape for _, shape in SCRATCH],
        compiler_params=pltpu.CompilerParams(
            collective_id=0, has_side_effects=True, vmem_limit_bytes=60 << 20
        ),
        cost_estimate=pl.CostEstimate(flops=12_000_000_000, bytes_accessed=16 << 20, transcendentals=0),
    )(
        query, out_grad, attention_out, log_norm.T, key, value,
        span_order, span_segment, key_weight, value_weight,
    )


def solution(mesh):
    split = P("ctx", "head")
    in_specs = (split,) * 6 + (P("ctx"), P("ctx"), P(None, "head"), P(None, "head"))
    return jax.shard_map(
        per_device, mesh=mesh, in_specs=in_specs, out_specs=(split,) * 4, check_vma=False
    )
```

```python
import math

import jax
import jax.numpy as jnp
from jax import lax
from jax.experimental import pallas as pl
from jax.experimental.pallas import tpu as pltpu
from jax.sharding import PartitionSpec as P

HEAD_DIM = 128
SPAN = 128
GROUP = 8
SCALE = 1.0 / math.sqrt(HEAD_DIM)
LOG2E = math.log2(math.e)
HIDDEN = -1e30
MESH = pl.DeviceIdType.MESH
F32, BF16, I32 = jnp.float32, jnp.bfloat16, jnp.int32
NN = (((1,), (0,)), ((), ()))
NT = (((1,), (1,)), ((), ()))
PIECE = 4 * SPAN
STEPS = 5
ENTRIES = 4 * STEPS
EMPTY, DIAG_HI, DIAG_LO = ENTRIES, ENTRIES + 1, ENTRIES + 2
AROUND = (1, 3, 2)


def dot(a, b, dims=NN):
    return lax.dot_general(a, b, dims, preferred_element_type=F32)


def kernel(q, do, o, norm, k, v, order, segment, wk, wv, dq_out, dk_out, dv_out, kg, wg, *scratch):
    names = [n for n, _ in SCRATCH]
    s = dict(zip(names, scratch))
    qs, ds = [s[f"qs{i}"] for i in range(4)], [s[f"ds{i}"] for i in range(4)]
    qt, dt = [s[f"qt{i}"] for i in range(4)], [s[f"dt{i}"] for i in range(4)]
    nrm, dlt = [s[f"nrm{i}"] for i in range(4)], [s[f"dlt{i}"] for i in range(4)]
    dqa = [s[f"dqa{i}"] for i in range(4)]
    nd = [s["nd0"], s["nd1"]]
    tab, tabz = s["tab"], s["tabz"]
    kbuf, vbuf, acck, accv = s["kbuf"], s["vbuf"], s["acck"], s["accv"]
    bk, bv = [s["bk0"], s["bk1"]], [s["bv0"], s["bv1"]]
    pos_lo, pos_hi, ent, vis, turn = s["pos_lo"], s["pos_hi"], s["ent"], s["vis"], s["turn"]

    ctx, head = lax.axis_index("ctx"), lax.axis_index("head")
    z, y, x = ctx // 16, (ctx // 4) % 4, ctx % 4
    me = y * 4 + x

    def at_x(d):
        return (z * 16 + y * 4 + (x + d) % 4, head)

    def at_y(d):
        return (z * 16 + ((y + d) % 4) * 4 + x, head)

    over = ((1 - z) * 16 + me, head)
    mate = head + 1 - 2 * (head % 2)
    far, far_mate = (head + 2) % 4, 3 - head
    weight_peers = ((ctx, mate), ((1 - z) * 16 + me, far), ((1 - z) * 16 + me, far_mate))
    head_peers = ((ctx, mate), (ctx, far), (ctx, far_mate))

    barrier = pltpu.get_barrier_semaphore()
    peers = [at_x(d) for d in AROUND] + [at_y(d) for d in AROUND] + [over]
    peers += [weight_peers[0], weight_peers[1], weight_peers[2], head_peers[1], head_peers[2]]
    for peer in peers:
        pl.semaphore_signal(barrier, inc=1, device_id=peer, device_id_type=MESH)

    sent = []

    def copy(src, dst, send, recv, peer):
        return pltpu.make_async_remote_copy(
            src_ref=src, dst_ref=dst, send_sem=send, recv_sem=recv, device_id=peer, device_id_type=MESH
        )

    def push(src, dst, send, recv, peer):
        c = copy(src, dst, send, recv, peer)
        c.start()
        sent.append(c)

    def arrived(dst, send, recv):
        copy(dst, dst, send, recv, over).wait_recv()

    def swapped(sel, first, second):
        shape = first.shape
        turn_round = jnp.full(shape, order[0], I32) > jnp.full(shape, order[1], I32)
        return jnp.where(turn_round, second, first) if sel == 0 else jnp.where(turn_round, first, second)

    slots = (pl.ds(0, SPAN), pl.ds(SPAN, SPAN))

    for sel in range(2):
        kbuf[2 * me + sel] = swapped(sel, k[slots[0], :], k[slots[1], :])
        vbuf[2 * me + sel] = swapped(sel, v[slots[0], :], v[slots[1], :])
    for i, value in enumerate((order[0], order[1], segment[0], segment[1])):
        tab[me, 0, i] = value

    def stack(p):
        for sel in range(2):
            for hh in range(4):
                r = pl.ds(hh * SPAN, SPAN)
                c = pl.ds((p * 4 + hh) * HEAD_DIM, HEAD_DIM)
                qs[p][sel, r, :] = swapped(sel, q[slots[0], c], q[slots[1], c])
                ds[p][sel, r, :] = swapped(sel, do[slots[0], c], do[slots[1], c])

    stack(0)
    stack(1)
    pl.semaphore_wait(barrier, len(peers))

    ks, vs = s["k_send"], s["v_send"]
    kr, vr = s["k_recv"], s["v_recv"]
    own = pl.ds(2 * me, 2)
    ms, mr, mrow = s["m_send"], s["m_recv"], s["m_row"]
    for i, d in enumerate(AROUND):
        push(tab.at[me], tab.at[me], ms.at[i], mr.at[me], at_x(d))
    for i, d in enumerate(AROUND):
        push(kbuf.at[own], kbuf.at[own], ks.at[i], kr.at[me], at_x(d))
        push(vbuf.at[own], vbuf.at[own], vs.at[i], vr.at[me], at_y(d))
    zs, zr = s["z_send"], s["z_recv"]
    push(tab.at[me], tabz.at[0], ms.at[6], s["mz_recv"].at[0], over)
    push(qs[0], qs[2], zs.at[0], zr.at[0], over)
    push(ds[0], ds[2], zs.at[1], zr.at[1], over)
    for i, d in enumerate(AROUND):
        push(kbuf.at[own], kbuf.at[own], ks.at[3 + i], kr.at[me], at_y(d))
        push(vbuf.at[own], vbuf.at[own], vs.at[3 + i], vr.at[me], at_x(d))
    ws, wr = s["w_send"], s["w_recv"]
    fill = []
    for i, w in enumerate((wk, wv)):
        columns = w.shape[0] // 4
        for j, peer in enumerate(weight_peers):
            rows = pl.ds(pl.multiple_of(peer[1] * columns, columns), columns)
            push(w.at[rows], wg.at[i, head], ws.at[3 * i + j], wr.at[4 * i + head], peer)
        rows = pl.ds(pl.multiple_of(head * columns, columns), columns)
        fill.append(pltpu.make_async_copy(w.at[rows], wg.at[i, head], s["fill"].at[i]))
        fill[-1].start()

    lane = lax.broadcasted_iota(I32, (2 * SPAN, 128), 1)
    sums = jnp.zeros((2 * SPAN, 128), F32)
    for h in range(GROUP):
        c = pl.ds(h * HEAD_DIM, HEAD_DIM)
        term = jnp.sum(do[:, c].astype(F32) * o[:, c].astype(F32), axis=1, keepdims=True)
        sums = jnp.where(lane == h, term, sums)
    sums = sums.T[0:8, :]
    for sel in range(2):
        c = pl.ds(sel * SPAN, SPAN)
        nd[0][0:8, c] = swapped(sel, norm[:, slots[0]], norm[:, slots[1]])
        nd[0][8:16, c] = swapped(sel, sums[:, :SPAN], sums[:, SPAN:])
    push(nd[0], nd[1], zs.at[2], zr.at[2], over)
    push(qs[1], qs[3], zs.at[3], zr.at[3], over)
    push(ds[1], ds[3], zs.at[4], zr.at[4], over)

    def spread(g):
        rows = jnp.concatenate([nd[g][...], jnp.zeros((112, 2 * SPAN), F32)], axis=0).T
        for p in range(2):
            for sel in range(2):
                part = rows[sel * SPAN : (sel + 1) * SPAN, :]
                for hh in range(4):
                    h, r = p * 4 + hh, pl.ds(hh * SPAN, SPAN)
                    nrm[2 * g + p][sel, r, :] = jnp.broadcast_to(part[:, h : h + 1] * LOG2E, (SPAN, 128))
                    dlt[2 * g + p][sel, r, :] = jnp.broadcast_to(part[:, 8 + h : 9 + h], (SPAN, 128))

    def turned(i):
        for sel in range(2):
            for hh in range(4):
                r = pl.ds(hh * SPAN, SPAN)
                qt[i][sel, :, r] = qs[i][sel, r, :].T
                dt[i][sel, :, r] = ds[i][sel, r, :].T

    def step(i, sel, k4, v4, bias=None, mask=None):
        n = k4.shape[0] // 128
        e = dot(qs[i][sel], k4, NT) * (SCALE * LOG2E) - jnp.concatenate([nrm[i][sel]] * n, axis=1)
        if bias is not None:
            e = e + bias
        if mask is not None:
            e = jnp.where(mask, e, HIDDEN)
        attend = jnp.exp2(e)
        grad = dot(ds[i][sel], v4, NT) - jnp.concatenate([dlt[i][sel]] * n, axis=1)
        score = (attend * grad).astype(BF16)
        return score, dot(qt[i][sel], score), dot(dt[i][sel], attend.astype(BF16))

    def bias_row(seen):
        return jnp.concatenate(
            [jnp.where(jnp.full((1, 128), one, I32) > 0, 0.0, HIDDEN) for one in seen], axis=1
        )

    def columns_of(a, u):
        return a[:, u * 128 : (u + 1) * 128]

    spread(0)
    turned(0)
    turned(1)
    for i, d in enumerate(AROUND):
        arrived(tab.at[y * 4 + (x + 4 - d) % 4], ms.at[0], mr.at[y * 4 + (x + 4 - d) % 4])
    for i, d in enumerate(AROUND):
        line = pl.ds(y * 4, 4)
        push(tab.at[line], tab.at[line], ms.at[3 + i], mrow.at[y], at_y(d))
    for i, d in enumerate(AROUND):
        j = y * 4 + (x + 4 - d) % 4
        two = pl.ds(2 * j, 2)
        arrived(kbuf.at[two], ks.at[0], kr.at[j])
        for n, e in enumerate(AROUND):
            push(kbuf.at[two], kbuf.at[two], ks.at[6 + 3 * i + n], kr.at[j], at_y(e))
        j = ((y + 4 - d) % 4) * 4 + x
        two = pl.ds(2 * j, 2)
        arrived(vbuf.at[two], vs.at[0], vr.at[j])
        for n, e in enumerate(AROUND):
            push(vbuf.at[two], vbuf.at[two], vs.at[6 + 3 * i + n], vr.at[j], at_x(e))

    row = lax.broadcasted_iota(I32, (PIECE, 128), 0) % SPAN
    below = lax.broadcasted_iota(I32, (PIECE, 128), 1) <= row
    for sel in range(2):
        k1, v1 = kbuf[2 * me + sel], vbuf[2 * me + sel]
        place = DIAG_HI if sel else DIAG_LO
        score, dk0, dv0 = step(0, sel, k1, v1, mask=below)
        dqa[0][sel] = dot(score, k1)
        score, dk1, dv1 = step(1, sel, k1, v1, mask=below)
        dqa[1][sel] = dot(score, k1)
        bk[0][place] = dk0 + dk1
        bv[0][place] = dv0 + dv1
    for g in range(2):
        bk[g][EMPTY] = jnp.zeros((128, 128), F32)
        bv[g][EMPTY] = jnp.zeros((128, 128), F32)
    for i in (2, 3):
        dqa[i][...] = jnp.zeros_like(dqa[i])

    def low_span(j):
        return jnp.minimum(tab[j, 0, 0], tab[j, 0, 1])

    def query_spans(t, j):
        first = t[j, 0, 0] < t[j, 0, 1]
        low = jnp.where(first, t[j, 0, 0], t[j, 0, 1])
        return low, jnp.where(first, t[j, 0, 2], t[j, 0, 3]), jnp.where(first, t[j, 0, 3], t[j, 0, 2])

    def later_rows(pieces, r, seg_hi, fresh):
        j0 = ((y + r) % 4) * 4
        k4 = jnp.concatenate([kbuf[2 * (j0 + u)] for u in range(4)], axis=0)
        v4 = jnp.concatenate([vbuf[2 * (j0 + u)] for u in range(4)], axis=0)
        bias = bias_row([low_span(j0 + u) - seg_hi + 1 for u in range(4)])
        dks = dvs = None
        for i in pieces:
            score, dk, dv = step(i, 1, k4, v4, bias=bias)
            dqa[i][1] += dot(score, k4)
            dks, dvs = (dk, dv) if dks is None else (dks + dk, dvs + dv)
        for u in range(4):
            if fresh:
                acck[j0 + u] = columns_of(dks, u)
                accv[j0 + u] = columns_of(dvs, u)
            else:
                acck[j0 + u] += columns_of(dks, u)
                accv[j0 + u] += columns_of(dvs, u)

    def sorted_rows(pieces, g, t, fresh):
        sel = jnp.where(t >= turn[g], 1, 0)
        k4 = jnp.concatenate([kbuf[ent[g * ENTRIES + 4 * t + u]] for u in range(4)], axis=0)
        v4 = jnp.concatenate([vbuf[ent[g * ENTRIES + 4 * t + u]] for u in range(4)], axis=0)
        bias = bias_row([vis[g * ENTRIES + 4 * t + u] for u in range(4)])
        none = jnp.zeros_like(k4)
        early = jnp.full(k4.shape, sel, I32) == 0
        wide = jnp.concatenate([jnp.where(early, k4, none), jnp.where(early, none, k4)], axis=1)
        dks = dvs = None
        for i in pieces:
            score, dk, dv = step(i, sel, k4, v4, bias=bias)
            both = dot(score, wide)
            dqa[i][0] += both[:, :128]
            dqa[i][1] += both[:, 128:]
            dks, dvs = (dk, dv) if dks is None else (dks + dk, dvs + dv)
        for u in range(4):
            if fresh:
                bk[g][4 * t + u] = columns_of(dks, u)
                bv[g][4 * t + u] = columns_of(dvs, u)
            else:
                bk[g][4 * t + u] += columns_of(dks, u)
                bv[g][4 * t + u] += columns_of(dvs, u)

    lo_own, seg_lo_own, seg_hi_own = query_spans(tab, me)
    for r in range(1, 4):
        arrived(tab.at[pl.ds(((y + r) % 4) * 4, 4)], ms.at[0], mrow.at[(y + r) % 4])
    arrived(tabz.at[0], ms.at[0], s["mz_recv"].at[0])
    lo_over, seg_lo_over, seg_hi_over = query_spans(tabz, 0)
    for g, (low, seg_lo, seg_hi) in enumerate(
        ((lo_own, seg_lo_own, seg_hi_own), (lo_over, seg_lo_over, seg_hi_over))
    ):
        spans = [low_span(j) for j in range(16)]
        before = sum(jnp.where(one < low, 1, 0) for one in spans)
        upto = sum(jnp.where(one <= low, 1, 0) for one in spans)
        first = (before + 3) // 4
        turn[g] = first

        def place(j, _, g=g, low=low, spans=spans, upto=upto, first=first):
            mine = low_span(j)
            rank = sum(jnp.where(one < mine, 1, 0) for one in spans)
            hi = 4 * first + rank - upto
            pos_lo[16 * g + j] = jnp.where(mine < low, rank, jnp.where(mine == low, DIAG_LO, EMPTY))
            pos_hi[16 * g + j] = jnp.where(mine > low, hi, jnp.where(mine == low, DIAG_HI, EMPTY))
            return 0

        lax.fori_loop(0, 16, place, 0)

        def entry(p, _, g=g, spans=spans, first=first, seg_lo=seg_lo, seg_hi=seg_hi):
            index, span = jnp.int32(0), jnp.int32(-1)
            for j in range(16):
                is_lo, is_hi = pos_lo[16 * g + j] == p, pos_hi[16 * g + j] == p
                index = jnp.where(is_lo, 2 * j, jnp.where(is_hi, 2 * j + 1, index))
                span = jnp.where(is_lo, spans[j], jnp.where(is_hi, 63 - spans[j], span))
            seg = jnp.where(p < 4 * first, seg_lo, seg_hi)
            ent[g * ENTRIES + p] = index
            vis[g * ENTRIES + p] = jnp.where(span >= seg, 1, 0)
            return 0

        lax.fori_loop(0, ENTRIES, entry, 0)

    def own_line(r, _):
        j0 = ((y + r) % 4) * 4
        for u in range(4):
            j = j0 + u
            two = pl.ds(2 * j, 2)

            @pl.when(r > 0)
            def _():
                arrived(kbuf.at[two], ks.at[0], kr.at[j])

            @pl.when(x != u)
            def _():
                arrived(vbuf.at[two], vs.at[0], vr.at[j])

        later_rows((0, 1), r, seg_hi_own, True)
        return 0

    lax.fori_loop(0, 4, own_line, 0)

    def own_sorted(t, _):
        sorted_rows((0, 1), 0, t, True)
        return 0

    lax.fori_loop(0, STEPS, own_sorted, 0)

    dqs, dqr = [s["dqs0"], s["dqs1"]], [s["dqr0"], s["dqr1"]]
    arrived(nd[1], zs.at[0], zr.at[2])
    spread(1)
    for p in range(2):
        i = 2 + p
        arrived(qs[i], zs.at[0], zr.at[3 * p])
        arrived(ds[i], zs.at[0], zr.at[3 * p + 1])
        turned(i)

        def over_sorted(t, _, i=i, p=p):
            sorted_rows((i,), 1, t, p == 0)
            return 0

        lax.fori_loop(0, STEPS, over_sorted, 0)

    def total(acc, b, j):
        lo = acc[j] + b[0][pos_lo[j]] + b[1][pos_lo[16 + j]]
        hi = b[0][pos_hi[j]] + b[1][pos_hi[16 + j]]
        return jnp.concatenate([lo, hi], axis=1).astype(BF16)

    sk, sv, r1k, r1v = s["sk"], s["sv"], s["r1k"], s["r1v"]
    s1k, s1v, s1kr, s1vr = s["s1k"], s["s1v"], s["s1kr"], s["s1vr"]

    def key_copy(d):
        yd = (y + d) % 4
        return copy(sk.at[pl.ds(yd * 4, 4)], r1k.at[d - 1], s1k.at[d - 1], s1kr.at[d - 1], at_y(d))

    def value_copy(d, line):
        n = (d - 1) * 4 + line
        return copy(sv.at[(x + d) % 4 * 4 + line], r1v.at[d - 1, line], s1v.at[n], s1vr.at[n], at_x(d))

    def over_line(r, _):
        line = (y + r + 1) % 4
        later_rows((2, 3), r + 1, seg_hi_over, False)
        for u in range(4):
            sk[line * 4 + u] = total(acck, bk, line * 4 + u)
            sv[u * 4 + line] = total(accv, bv, line * 4 + u)

        @pl.when(r < 3)
        def _():
            key_copy(r + 1).start()

        for d in AROUND:
            value_copy(d, line).start()
        return 0

    lax.fori_loop(0, 4, over_line, 0)
    for p in range(2):
        dqs[p][...] = dqa[2 + p][...].astype(BF16)
        push(dqs[p], dqr[p], zs.at[5 + p], zr.at[5 + p], over)

    t2k, t2v, r2k, r2v = s["t2k"], s["t2v"], s["r2k"], s["r2v"]
    for d in (1, 2, 3):
        key_copy(d).wait_recv()

    def sum_keys(u, _):
        parts = sk[y * 4 + u].astype(F32) + r1k[0, u].astype(F32)
        t2k[u] = (parts + r1k[1, u].astype(F32) + r1k[2, u].astype(F32)).astype(BF16)
        return 0

    lax.fori_loop(0, 4, sum_keys, 0)
    for i, d in enumerate(AROUND):
        push(t2k.at[(x + d) % 4], r2k.at[d - 1], s["s2"].at[i], s["s2r"].at[d - 1], at_x(d))

    def value_back(d):
        return copy(t2v.at[(y + d) % 4], r2v.at[d - 1], s["s2"].at[2 + d], s["s2r"].at[2 + d], at_y(d))

    def sum_values(r, _):
        line = (y + r + 1) % 4
        for d in AROUND:
            value_copy(d, line).wait_recv()
        parts = sv[x * 4 + line].astype(F32) + r1v[0, line].astype(F32)
        t2v[line] = (parts + r1v[1, line].astype(F32) + r1v[2, line].astype(F32)).astype(BF16)

        @pl.when(r < 3)
        def _():
            value_back(r + 1).start()

        return 0

    lax.fori_loop(0, 4, sum_values, 0)

    for p in range(2):
        arrived(dqr[p], zs.at[0], zr.at[5 + p])
        for hh in range(4):
            r, c = pl.ds(hh * SPAN, SPAN), pl.ds((p * 4 + hh) * HEAD_DIM, HEAD_DIM)
            both = [(dqa[p][sel, r, :] + dqr[p][sel, r, :].astype(F32)) * SCALE for sel in range(2)]
            for slot in range(2):
                dq_out[slots[slot], c] = swapped(slot, both[0], both[1]).astype(BF16)

    fin = s["fin"]
    for w, (t2, r2, mine, out, scale) in enumerate(
        ((t2k, r2k, x, dk_out, SCALE), (t2v, r2v, y, dv_out, 1.0))
    ):
        for d in range(3):
            arrived(r2.at[d], s["s2"].at[0], s["s2r"].at[3 * w + d])
        whole = t2[mine].astype(F32) + r2[0].astype(F32) + r2[1].astype(F32) + r2[2].astype(F32)
        both = [(columns_of(whole, sel) * scale).T for sel in range(2)]
        for slot in range(2):
            low = swapped(slot, both[0], both[1]).astype(BF16)
            out[slots[slot], :] = low
            fin[w, slots[slot], :] = low
        fill.append(pltpu.make_async_copy(fin.at[w], kg.at[w, head], s["fill"].at[2 + w]))
        fill[-1].start()
        for i, peer in enumerate(head_peers):
            push(fin.at[w], kg.at[w, head], s["g_send"].at[3 * w + i], s["g_recv"].at[4 * w + head], peer)

    for w in range(2):
        for h in (mate, far, far_mate):
            arrived(wg.at[w, h], ws.at[0], wr.at[4 * w + h])
            arrived(kg.at[w, h], ws.at[0], s["g_recv"].at[4 * w + h])
    for c in fill:
        c.wait()
    for c in sent:
        c.wait_send()
    for d in (1, 2, 3):
        key_copy(d).wait_send()
        value_back(d).wait_send()
        for line in range(4):
            value_copy(d, line).wait_send()


TILES = 8


def finish(dq, dk, dv, kg, wg, dq_out, dk_out, dv_out, ig_out, a, b, c, dq_in, dk_in, dv_in, into, out, through):
    handed = ((dq, dq_in, dq_out), (dk, dk_in, dk_out), (dv, dv_in, dv_out))
    inward = [pltpu.make_async_copy(src, via, through.at[i]) for i, (src, via, _) in enumerate(handed)]
    onward = [pltpu.make_async_copy(via, dst, through.at[3 + i]) for i, (_, via, dst) in enumerate(handed)]
    first = pltpu.make_async_copy(kg, a, into.at[TILES])
    first.start()
    cols = b.shape[2] // TILES
    loads = [
        pltpu.make_async_copy(wg.at[:, :, pl.ds(n * cols, cols)], b.at[:, :, pl.ds(n * cols, cols)], into.at[n])
        for n in range(TILES)
    ]
    for one in loads + inward:
        one.start()
    first.wait()
    stores = []
    for n in range(TILES):
        loads[n].wait()
        r = pl.ds(n * cols, cols)
        acc = None
        for w in range(2):
            for h in (0, 2):
                left = jnp.concatenate([a[w, h], a[w, h + 1]], axis=1)
                right = jnp.concatenate([b[w, h, r, :], b[w, h + 1, r, :]], axis=1)
                term = dot(left, right, NT)
                acc = term if acc is None else acc + term
        c[:, r] = acc.astype(BF16)
        stores.append(pltpu.make_async_copy(c.at[:, r], ig_out.at[:, r], out.at[n]))
        stores[-1].start()
        if n < 3:
            inward[n].wait()
            onward[n].start()
    for one in stores + onward:
        one.wait()


def _scratch():
    v, dma, smem = pltpu.VMEM, pltpu.SemaphoreType.DMA, pltpu.SMEM
    out = []
    for i in range(4):
        out += [(f"qs{i}", v((2, PIECE, 128), BF16)), (f"ds{i}", v((2, PIECE, 128), BF16))]
        out += [(f"qt{i}", v((2, 128, PIECE), BF16)), (f"dt{i}", v((2, 128, PIECE), BF16))]
        out += [(f"nrm{i}", v((2, PIECE, 128), F32)), (f"dlt{i}", v((2, PIECE, 128), F32))]
        out += [(f"dqa{i}", v((2, PIECE, 128), F32))]
    for i in range(2):
        out += [(f"nd{i}", v((16, 256), F32)), (f"dqs{i}", v((2, PIECE, 128), BF16))]
        out += [(f"dqr{i}", v((2, PIECE, 128), BF16))]
        out += [(f"bk{i}", v((ENTRIES + 3, 128, 128), F32)), (f"bv{i}", v((ENTRIES + 3, 128, 128), F32))]
    out += [("tab", smem((16, 1, 128), I32)), ("tabz", smem((1, 1, 128), I32))]
    out += [("kbuf", v((32, 128, 128), BF16)), ("vbuf", v((32, 128, 128), BF16))]
    out += [("acck", v((16, 128, 128), F32)), ("accv", v((16, 128, 128), F32))]
    out += [("pos_lo", smem((32,), I32)), ("pos_hi", smem((32,), I32)), ("ent", smem((2 * ENTRIES,), I32))]
    out += [("vis", smem((2 * ENTRIES,), I32)), ("turn", smem((2,), I32))]
    out += [("sk", v((16, 128, 256), BF16)), ("sv", v((16, 128, 256), BF16))]
    for n in ("k", "v"):
        out += [(f"r1{n}", v((3, 4, 128, 256), BF16))]
        out += [(f"t2{n}", v((4, 128, 256), BF16)), (f"r2{n}", v((3, 128, 256), BF16))]
    out += [("fin", v((2, 256, 128), BF16))]
    out += [("k_send", dma((15,))), ("v_send", dma((15,))), ("k_recv", dma((16,))), ("v_recv", dma((16,)))]
    out += [("m_send", dma((7,))), ("m_recv", dma((16,))), ("m_row", dma((4,))), ("mz_recv", dma((1,)))]
    out += [("z_send", dma((7,))), ("z_recv", dma((7,))), ("w_send", dma((6,))), ("w_recv", dma((8,)))]
    out += [("fill", dma((4,))), ("s1k", dma((3,))), ("s1kr", dma((3,))), ("s1v", dma((12,))), ("s1vr", dma((12,)))]
    out += [("s2", dma((6,))), ("s2r", dma((6,)))]
    out += [("g_send", dma((6,))), ("g_recv", dma((8,)))]
    return out


SCRATCH = _scratch()


def per_device(
    query, key, value, attention_out, out_grad, log_norm, span_order, span_segment, key_weight, value_weight
):
    rows = query.shape[0]
    vmem, smem = pl.BlockSpec(memory_space=pltpu.VMEM), pl.BlockSpec(memory_space=pltpu.SMEM)
    hbm = pl.BlockSpec(memory_space=pl.ANY)
    columns = key_weight.shape[0] // 4
    small = (
        jax.ShapeDtypeStruct(query.shape, BF16),
        jax.ShapeDtypeStruct(key.shape, BF16),
        jax.ShapeDtypeStruct(value.shape, BF16),
    )
    held = pl.pallas_call(
        kernel,
        name="attention_backward",
        out_shape=small
        + (
            jax.ShapeDtypeStruct((2, 4, rows, HEAD_DIM), BF16),
            jax.ShapeDtypeStruct((2, 4, columns, HEAD_DIM), BF16),
        ),
        in_specs=[vmem] * 6 + [smem] * 2 + [hbm] * 2,
        out_specs=(vmem,) * 3 + (hbm,) * 2,
        scratch_shapes=[shape for _, shape in SCRATCH],
        compiler_params=pltpu.CompilerParams(
            collective_id=0, has_side_effects=True, vmem_limit_bytes=60 << 20
        ),
        cost_estimate=pl.CostEstimate(flops=11_000_000_000, bytes_accessed=16 << 20, transcendentals=0),
    )(
        query, out_grad, attention_out, log_norm.T, key, value,
        span_order, span_segment, key_weight, value_weight,
    )
    dma = pltpu.SemaphoreType.DMA
    return pl.pallas_call(
        finish,
        name="input_gradient",
        out_shape=small + (jax.ShapeDtypeStruct((rows, columns), BF16),),
        in_specs=[hbm] * 5,
        out_specs=(hbm,) * 4,
        scratch_shapes=[
            pltpu.VMEM((2, 4, rows, HEAD_DIM), BF16),
            pltpu.VMEM((2, 4, columns, HEAD_DIM), BF16),
            pltpu.VMEM((rows, columns), BF16),
            pltpu.VMEM(query.shape, BF16),
            pltpu.VMEM(key.shape, BF16),
            pltpu.VMEM(value.shape, BF16),
            dma((TILES + 1,)),
            dma((TILES,)),
            dma((6,)),
        ],
        compiler_params=pltpu.CompilerParams(vmem_limit_bytes=60 << 20),
        cost_estimate=pl.CostEstimate(flops=1_100_000_000, bytes_accessed=8 << 20, transcendentals=0),
    )(*held)


def solution(mesh):
    split = P("ctx", "head")
    in_specs = (split,) * 6 + (P("ctx"), P("ctx"), P(None, "head"), P(None, "head"))
    return jax.shard_map(
        per_device, mesh=mesh, in_specs=in_specs, out_specs=(split,) * 4, check_vma=False
    )
```

```python
import math

import jax
import jax.numpy as jnp
from jax import lax
from jax.experimental import pallas as pl
from jax.experimental.pallas import tpu as pltpu
from jax.sharding import PartitionSpec as P

HEAD_DIM = 128
SPAN = 128
GROUP = 8
SCALE = 1.0 / math.sqrt(HEAD_DIM)
LOG2E = math.log2(math.e)
HIDDEN = -1e30
MESH = pl.DeviceIdType.MESH
F32, BF16, I32 = jnp.float32, jnp.bfloat16, jnp.int32
NN = (((1,), (0,)), ((), ()))
NT = (((1,), (1,)), ((), ()))
PIECE = 4 * SPAN
STEPS = 3
ENTRIES = 4 * STEPS
EMPTY, DIAG_HI, DIAG_LO = ENTRIES, ENTRIES + 1, ENTRIES + 2
AROUND = (1, 3, 2)


def dot(a, b, dims=NN):
    return lax.dot_general(a, b, dims, preferred_element_type=F32)


def kernel(q, do, o, norm, k, v, order, segment, wk, wv, dq_out, dk_out, dv_out, kg, wg, *scratch):
    names = [n for n, _ in SCRATCH]
    s = dict(zip(names, scratch))
    qs, ds = [s[f"qs{i}"] for i in range(4)], [s[f"ds{i}"] for i in range(4)]
    qt, dt = [s[f"qt{i}"] for i in range(4)], [s[f"dt{i}"] for i in range(4)]
    nrm, dlt = [s[f"nrm{i}"] for i in range(4)], [s[f"dlt{i}"] for i in range(4)]
    dqa = [s[f"dqa{i}"] for i in range(4)]
    nd = [s["nd0"], s["nd1"]]
    tab, tabz = s["tab"], s["tabz"]
    kb, vb, acck, accv = [s["kb0"], s["kb1"]], [s["vb0"], s["vb1"]], s["acck"], s["accv"]
    bk = [[s[f"bk{g}{half}"] for half in range(2)] for g in range(2)]
    bv = [[s[f"bv{g}{half}"] for half in range(2)] for g in range(2)]
    pos_lo, pos_hi, ent, vis, turn = s["pos_lo"], s["pos_hi"], s["ent"], s["vis"], s["turn"]

    ctx, head = lax.axis_index("ctx"), lax.axis_index("head")
    z, y, x = ctx // 16, (ctx // 4) % 4, ctx % 4
    me = y * 4 + x

    def at_x(d):
        return (z * 16 + y * 4 + (x + d) % 4, head)

    def at_y(d):
        return (z * 16 + ((y + d) % 4) * 4 + x, head)

    over = ((1 - z) * 16 + me, head)
    mate = head + 1 - 2 * (head % 2)
    far, far_mate = (head + 2) % 4, 3 - head
    weight_peers = ((ctx, mate), ((1 - z) * 16 + me, far), ((1 - z) * 16 + me, far_mate))

    barrier = pltpu.get_barrier_semaphore()
    peers = [at_x(d) for d in AROUND] + [at_y(d) for d in AROUND] + [over]
    peers += [weight_peers[0], weight_peers[1], weight_peers[2], (ctx, far)]
    for peer in peers:
        pl.semaphore_signal(barrier, inc=1, device_id=peer, device_id_type=MESH)

    sent = []

    def copy(src, dst, send, recv, peer):
        return pltpu.make_async_remote_copy(
            src_ref=src, dst_ref=dst, send_sem=send, recv_sem=recv, device_id=peer, device_id_type=MESH
        )

    def push(src, dst, send, recv, peer):
        c = copy(src, dst, send, recv, peer)
        c.start()
        sent.append(c)

    def arrived(dst, send, recv):
        copy(dst, dst, send, recv, over).wait_recv()

    def swapped(sel, first, second):
        shape = first.shape
        turn_round = jnp.full(shape, order[0], I32) > jnp.full(shape, order[1], I32)
        return jnp.where(turn_round, second, first) if sel == 0 else jnp.where(turn_round, first, second)

    slots = (pl.ds(0, SPAN), pl.ds(SPAN, SPAN))

    for sel in range(2):
        kb[0][2 * x + sel] = swapped(sel, k[slots[0], :], k[slots[1], :])
        vb[0][2 * x + sel] = swapped(sel, v[slots[0], :], v[slots[1], :])
    for i, value in enumerate((order[0], order[1], segment[0], segment[1])):
        tab[me, 0, i] = value

    def stack(p):
        for sel in range(2):
            for hh in range(4):
                r = pl.ds(hh * SPAN, SPAN)
                c = pl.ds((p * 4 + hh) * HEAD_DIM, HEAD_DIM)
                qs[p][sel, r, :] = swapped(sel, q[slots[0], c], q[slots[1], c])
                ds[p][sel, r, :] = swapped(sel, do[slots[0], c], do[slots[1], c])

    stack(0)
    stack(1)
    pl.semaphore_wait(barrier, len(peers))

    ks, vs = s["k_send"], s["v_send"]
    kr, vr = s["k_recv"], s["v_recv"]
    ms, mr, mrow = s["m_send"], s["m_recv"], s["m_row"]

    def block(buf, r, u):
        return buf[r // 2].at[pl.ds(2 * (r % 2 * 4 + u), 2)]

    def along_x(buf, r, u, send, recv, d):
        push(block(buf, r, u), block(buf, r, u), send, recv.at[r * 4 + u], at_x(d))

    def along_y(buf, r, u, send, recv, d):
        there = (r + 4 - d) % 4
        push(block(buf, r, u), block(buf, there, u), send, recv.at[there * 4 + u], at_y(d))

    for i, d in enumerate(AROUND):
        push(tab.at[me], tab.at[me], ms.at[i], mr.at[me], at_x(d))
    for i, d in enumerate((1, 3)):
        along_x(kb, 0, x, ks.at[i], kr, d)
        along_y(vb, 0, x, vs.at[i], vr, d)
    along_x(kb, 0, x, ks.at[2], kr, 2)
    for i, d in enumerate(AROUND):
        along_x(vb, 0, x, vs.at[3 + i], vr, d)
    for i, d in enumerate((3, 1)):
        along_y(kb, 0, x, ks.at[3 + i], kr, d)
    zs, zr = s["z_send"], s["z_recv"]
    push(tab.at[me], tabz.at[0], ms.at[6], s["mz_recv"].at[0], over)
    push(qs[0], qs[2], zs.at[0], zr.at[0], over)
    push(ds[0], ds[2], zs.at[1], zr.at[1], over)
    ws, wr = s["w_send"], s["w_recv"]
    columns = wk.shape[0] // 4

    def weight_copy(i, w, j):
        peer = weight_peers[j]
        rows = pl.ds(pl.multiple_of(peer[1] * columns, columns), columns)
        return copy(w.at[rows], wg.at[i, head], ws.at[3 * i + j], wr.at[4 * i + head], peer)

    for i, w in enumerate((wk, wv)):
        for j in range(3):
            weight_copy(i, w, j).start()

    fill = []

    lane = lax.broadcasted_iota(I32, (2 * SPAN, 128), 1)
    sums = jnp.zeros((2 * SPAN, 128), F32)
    for h in range(GROUP):
        c = pl.ds(h * HEAD_DIM, HEAD_DIM)
        term = jnp.sum(do[:, c].astype(F32) * o[:, c].astype(F32), axis=1, keepdims=True)
        sums = jnp.where(lane == h, term, sums)
    sums = sums.T[0:8, :]
    for sel in range(2):
        c = pl.ds(sel * SPAN, SPAN)
        nd[0][0:8, c] = swapped(sel, norm[:, slots[0]], norm[:, slots[1]])
        nd[0][8:16, c] = swapped(sel, sums[:, :SPAN], sums[:, SPAN:])
    push(nd[0], nd[1], zs.at[2], zr.at[2], over)
    push(qs[1], qs[3], zs.at[3], zr.at[3], over)
    push(ds[1], ds[3], zs.at[4], zr.at[4], over)

    def spread(g):
        rows = jnp.concatenate([nd[g][...], jnp.zeros((112, 2 * SPAN), F32)], axis=0).T
        for p in range(2):
            for sel in range(2):
                part = rows[sel * SPAN : (sel + 1) * SPAN, :]
                for hh in range(4):
                    h, r = p * 4 + hh, pl.ds(hh * SPAN, SPAN)
                    nrm[2 * g + p][sel, r, :] = jnp.broadcast_to(part[:, h : h + 1] * LOG2E, (SPAN, 128))
                    dlt[2 * g + p][sel, r, :] = jnp.broadcast_to(part[:, 8 + h : 9 + h], (SPAN, 128))

    def turned(i):
        for sel in range(2):
            for hh in range(4):
                r = pl.ds(hh * SPAN, SPAN)
                qt[i][sel, :, r] = qs[i][sel, r, :].T
                dt[i][sel, :, r] = ds[i][sel, r, :].T

    def step(i, sel, k4, v4, bias=None, mask=None):
        n = k4.shape[0] // 128
        e = dot(qs[i][sel], k4, NT) * (SCALE * LOG2E) - jnp.concatenate([nrm[i][sel]] * n, axis=1)
        if bias is not None:
            e = e + bias
        if mask is not None:
            e = jnp.where(mask, e, HIDDEN)
        attend = jnp.exp2(e)
        grad = dot(ds[i][sel], v4, NT) - jnp.concatenate([dlt[i][sel]] * n, axis=1)
        score = (attend * grad).astype(BF16)
        return score, dot(qt[i][sel], score), dot(dt[i][sel], attend.astype(BF16))

    def bias_row(seen):
        return jnp.concatenate(
            [jnp.where(jnp.full((1, 128), one, I32) > 0, 0.0, HIDDEN) for one in seen], axis=1
        )

    def columns_of(a, u):
        return a[:, u * 128 : (u + 1) * 128]

    spread(0)
    turned(0)
    turned(1)
    for i, d in enumerate(AROUND):
        arrived(tab.at[y * 4 + (x + 4 - d) % 4], ms.at[0], mr.at[y * 4 + (x + 4 - d) % 4])
    for i, d in enumerate(AROUND):
        line = pl.ds(y * 4, 4)
        push(tab.at[line], tab.at[line], ms.at[3 + i], mrow.at[y], at_y(d))
    along_y(vb, 0, x, vs.at[2], vr, 2)
    for i, d in enumerate(AROUND):
        u = (x + 4 - d) % 4
        arrived(block(kb, 0, u), ks.at[0], kr.at[u])
        for n, e in enumerate((3, 1)):
            along_y(kb, 0, u, ks.at[6 + 3 * i + n], kr, e)
        if d != 2:
            r = (1, 3)[i]
            arrived(block(vb, r, x), vs.at[0], vr.at[4 * r + x])
            for n, e in enumerate(AROUND):
                along_x(vb, r, x, vs.at[6 + 3 * i + n], vr, e)

    def hand_on_last():
        along_y(kb, 0, x, ks.at[5], kr, 2)
        for i, d in enumerate(AROUND):
            along_y(kb, 0, (x + 4 - d) % 4, ks.at[8 + 3 * i], kr, 2)
        arrived(block(vb, 2, x), vs.at[0], vr.at[8 + x])
        for n, e in enumerate(AROUND):
            along_x(vb, 2, x, vs.at[12 + n], vr, e)

    row = lax.broadcasted_iota(I32, (PIECE, 128), 0) % SPAN
    below = lax.broadcasted_iota(I32, (PIECE, 128), 1) <= row
    for sel in range(2):
        k1, v1 = kb[0][2 * x + sel], vb[0][2 * x + sel]
        place = DIAG_HI if sel else DIAG_LO
        score, dk0, dv0 = step(0, sel, k1, v1, mask=below)
        dqa[0][sel] = dot(score, k1)
        score, dk1, dv1 = step(1, sel, k1, v1, mask=below)
        dqa[1][sel] = dot(score, k1)
        bk[0][0][place] = dk0 + dk1
        bv[0][0][place] = dv0 + dv1
    for b in (bk, bv):
        for g in range(2):
            for half in range(2):
                b[g][half][EMPTY] = jnp.zeros((128, 128), F32)
    for i in (2, 3):
        dqa[i][...] = jnp.zeros_like(dqa[i])

    def low_span(j):
        return jnp.minimum(tab[j, 0, 0], tab[j, 0, 1])

    def query_spans(t, j):
        first = t[j, 0, 0] < t[j, 0, 1]
        low = jnp.where(first, t[j, 0, 0], t[j, 0, 1])
        return low, jnp.where(first, t[j, 0, 2], t[j, 0, 3]), jnp.where(first, t[j, 0, 3], t[j, 0, 2])

    def device_at(half, n):
        return (y + 2 * half + n // 4) % 4 * 4 + n % 4

    def later_rows(pieces, half, line, seg_hi, fresh):
        k4 = jnp.concatenate([kb[half][8 * line + 2 * u] for u in range(4)], axis=0)
        v4 = jnp.concatenate([vb[half][8 * line + 2 * u] for u in range(4)], axis=0)
        bias = bias_row([low_span(device_at(half, 4 * line + u)) - seg_hi + 1 for u in range(4)])
        dks = dvs = None
        for i in pieces:
            score, dk, dv = step(i, 1, k4, v4, bias=bias)
            dqa[i][1] += dot(score, k4)
            dks, dvs = (dk, dv) if dks is None else (dks + dk, dvs + dv)
        for u in range(4):
            place = 8 * half + 4 * line + u
            if fresh:
                acck[place] = columns_of(dks, u)
                accv[place] = columns_of(dvs, u)
            else:
                acck[place] += columns_of(dks, u)
                accv[place] += columns_of(dvs, u)

    def sorted_rows(pieces, g, half, t):
        which = 2 * g + half
        sel = jnp.where(t >= turn[which], 1, 0)
        k4 = jnp.concatenate([kb[half][ent[which * ENTRIES + 4 * t + u]] for u in range(4)], axis=0)
        v4 = jnp.concatenate([vb[half][ent[which * ENTRIES + 4 * t + u]] for u in range(4)], axis=0)
        bias = bias_row([vis[which * ENTRIES + 4 * t + u] for u in range(4)])
        none = jnp.zeros_like(k4)
        early = jnp.full(k4.shape, sel, I32) == 0
        wide = jnp.concatenate([jnp.where(early, k4, none), jnp.where(early, none, k4)], axis=1)
        dks = dvs = None
        for i in pieces:
            score, dk, dv = step(i, sel, k4, v4, bias=bias)
            both = dot(score, wide)
            dqa[i][0] += both[:, :128]
            dqa[i][1] += both[:, 128:]
            dks, dvs = (dk, dv) if dks is None else (dks + dk, dvs + dv)
        for u in range(4):
            bk[g][half][4 * t + u] = columns_of(dks, u)
            bv[g][half][4 * t + u] = columns_of(dvs, u)

    lo_own, seg_lo_own, seg_hi_own = query_spans(tab, me)
    for r in range(1, 4):
        arrived(tab.at[pl.ds(((y + r) % 4) * 4, 4)], ms.at[0], mrow.at[(y + r) % 4])
    arrived(tabz.at[0], ms.at[0], s["mz_recv"].at[0])
    lo_over, seg_lo_over, seg_hi_over = query_spans(tabz, 0)
    for g, (low, seg_lo, seg_hi) in enumerate(
        ((lo_own, seg_lo_own, seg_hi_own), (lo_over, seg_lo_over, seg_hi_over))
    ):
        for half in range(2):
            which = 2 * g + half
            spans = [low_span(device_at(half, n)) for n in range(8)]
            before = sum(jnp.where(one < low, 1, 0) for one in spans)
            upto = sum(jnp.where(one <= low, 1, 0) for one in spans)
            first = (before + 3) // 4
            turn[which] = first

            def place(n, _, half=half, which=which, low=low, spans=spans, upto=upto, first=first):
                mine = low_span(device_at(half, n))
                rank = sum(jnp.where(one < mine, 1, 0) for one in spans)
                hi = 4 * first + rank - upto
                pos_lo[8 * which + n] = jnp.where(mine < low, rank, jnp.where(mine == low, DIAG_LO, EMPTY))
                pos_hi[8 * which + n] = jnp.where(mine > low, hi, jnp.where(mine == low, DIAG_HI, EMPTY))
                return 0

            lax.fori_loop(0, 8, place, 0)

            def entry(p, _, which=which, spans=spans, first=first, seg_lo=seg_lo, seg_hi=seg_hi):
                index, span = jnp.int32(0), jnp.int32(-1)
                for n in range(8):
                    is_lo, is_hi = pos_lo[8 * which + n] == p, pos_hi[8 * which + n] == p
                    index = jnp.where(is_lo, 2 * n, jnp.where(is_hi, 2 * n + 1, index))
                    span = jnp.where(is_lo, spans[n], jnp.where(is_hi, 63 - spans[n], span))
                seg = jnp.where(p < 4 * first, seg_lo, seg_hi)
                ent[which * ENTRIES + p] = index
                vis[which * ENTRIES + p] = jnp.where(span >= seg, 1, 0)
                return 0

            lax.fori_loop(0, ENTRIES, entry, 0)

    for half in range(2):

        def own_line(line, _, half=half):
            r = 2 * half + line
            for u in range(4):
                place = pl.ds(2 * (line * 4 + u), 2)

                if r > 0:
                    arrived(kb[half].at[place], ks.at[0], kr.at[4 * r + u])

                @pl.when(x != u)
                def _():
                    arrived(vb[half].at[place], vs.at[0], vr.at[4 * r + u])

            later_rows((0, 1), half, line, seg_hi_own, True)
            return 0

        if half == 0:
            own_line(0, 0)
            hand_on_last()
            own_line(1, 0)
        else:
            own_line(1, 0)
            own_line(0, 0)

        def own_sorted(t, _, half=half):
            sorted_rows((0, 1), 0, half, t)
            return 0

        lax.fori_loop(0, STEPS, own_sorted, 0)

    dqs, dqr = [s["dqs0"], s["dqs1"]], [s["dqr0"], s["dqr1"]]
    arrived(nd[1], zs.at[0], zr.at[2])
    spread(1)
    for p in range(2):
        arrived(qs[2 + p], zs.at[0], zr.at[3 * p])
        arrived(ds[2 + p], zs.at[0], zr.at[3 * p + 1])
        turned(2 + p)

    def total(acc, b, half, n):
        lo = acc[8 * half + n] + b[0][half][pos_lo[8 * half + n]] + b[1][half][pos_lo[16 + 8 * half + n]]
        hi = b[0][half][pos_hi[8 * half + n]] + b[1][half][pos_hi[16 + 8 * half + n]]
        return jnp.concatenate([lo, hi], axis=1).astype(BF16)

    sk, sv, r1k, r1v = s["sk"], s["sv"], s["r1k"], s["r1v"]
    s1k, s1v, s1kr, s1vr = s["s1k"], s["s1v"], s["s1kr"], s["s1vr"]

    def key_copy(d):
        return copy(sk.at[pl.ds(d * 4, 4)], r1k.at[d - 1], s1k.at[d - 1], s1kr.at[d - 1], at_y(d))

    def value_copy(d, r):
        n = (d - 1) * 4 + r
        return copy(sv.at[r * 4 + (x + d) % 4], r1v.at[d - 1, r], s1v.at[n], s1vr.at[n], at_x(d))

    for half in (1, 0):

        def over_sorted(t, _, half=half):
            sorted_rows((2, 3), 1, half, t)
            return 0

        lax.fori_loop(0, STEPS, over_sorted, 0)

        def over_line(i, _, half=half):
            line = i if half else 1 - i
            r = 2 * half + line
            later_rows((2, 3), half, line, seg_hi_over, False)
            for u in range(4):
                sk[r * 4 + u] = total(acck, bk, half, 4 * line + u)
                sv[r * 4 + u] = total(accv, bv, half, 4 * line + u)

            @pl.when(r > 0)
            def _():
                key_copy(r).start()

            for d in AROUND:
                value_copy(d, r).start()
            return 0

        lax.fori_loop(0, 2, over_line, 0)

    for p in range(2):
        dqs[p][...] = dqa[2 + p][...].astype(BF16)
        push(dqs[p], dqr[p], zs.at[5 + p], zr.at[5 + p], over)

    t2k, t2v, r2k, r2v = s["t2k"], s["t2v"], s["r2k"], s["r2v"]
    for d in (1, 2, 3):
        key_copy(d).wait_recv()

    def sum_keys(u, _):
        parts = sk[u].astype(F32) + r1k[0, u].astype(F32)
        t2k[u] = (parts + r1k[1, u].astype(F32) + r1k[2, u].astype(F32)).astype(BF16)
        return 0

    lax.fori_loop(0, 4, sum_keys, 0)
    for i, d in enumerate(AROUND):
        push(t2k.at[(x + d) % 4], r2k.at[d - 1], s["s2"].at[i], s["s2r"].at[d - 1], at_x(d))

    def value_back(d):
        return copy(t2v.at[d], r2v.at[d - 1], s["s2"].at[2 + d], s["s2r"].at[2 + d], at_y(d))

    def sum_values(i, _):
        r = jnp.where(i < 2, i + 2, 3 - i)
        for d in AROUND:
            value_copy(d, r).wait_recv()
        parts = sv[r * 4 + x].astype(F32) + r1v[0, r].astype(F32)
        t2v[r] = (parts + r1v[1, r].astype(F32) + r1v[2, r].astype(F32)).astype(BF16)

        @pl.when(r > 0)
        def _():
            value_back(r).start()

        return 0

    lax.fori_loop(0, 4, sum_values, 0)

    for p in range(2):
        arrived(dqr[p], zs.at[0], zr.at[5 + p])
        for hh in range(4):
            r, c = pl.ds(hh * SPAN, SPAN), pl.ds((p * 4 + hh) * HEAD_DIM, HEAD_DIM)
            both = [(dqa[p][sel, r, :] + dqr[p][sel, r, :].astype(F32)) * SCALE for sel in range(2)]
            for slot in range(2):
                dq_out[slots[slot], c] = swapped(slot, both[0], both[1]).astype(BF16)

    fin = s["fin"]
    for w, (t2, r2, mine, out, scale) in enumerate(
        ((t2k, r2k, x, dk_out, SCALE), (t2v, r2v, 0, dv_out, 1.0))
    ):
        for d in range(3):
            arrived(r2.at[d], s["s2"].at[0], s["s2r"].at[3 * w + d])
        whole = t2[mine].astype(F32) + r2[0].astype(F32) + r2[1].astype(F32) + r2[2].astype(F32)
        both = [(columns_of(whole, sel) * scale).T for sel in range(2)]
        for slot in range(2):
            low = swapped(slot, both[0], both[1]).astype(BF16)
            out[slots[slot], :] = low
            fin[w, slots[slot], :] = low
        fill.append(pltpu.make_async_copy(fin.at[w], kg.at[w, head], s["fill"].at[w]))
        fill[-1].start()
        for i, peer in enumerate(((ctx, far), (ctx, mate))):
            push(fin.at[w], kg.at[w, head], s["g_send"].at[3 * w + i], s["g_recv"].at[4 * w + head], peer)
    for w in range(2):
        arrived(kg.at[w, far], ws.at[0], s["g_recv"].at[4 * w + far])
        push(kg.at[w, far], kg.at[w, far], s["g_send"].at[3 * w + 2], s["g_recv"].at[4 * w + far], (ctx, mate))

    for w in range(2):
        for h in (mate, far_mate):
            arrived(kg.at[w, h], ws.at[0], s["g_recv"].at[4 * w + h])
        for j, h in enumerate((mate, far, far_mate)):
            arrived(wg.at[w, h], ws.at[0], wr.at[4 * w + h])
            weight_copy(w, (wk, wv)[w], j).wait_send()
    for c in fill:
        c.wait()
    for c in sent:
        c.wait_send()
    for d in (1, 2, 3):
        key_copy(d).wait_send()
        value_back(d).wait_send()
        for r in range(4):
            value_copy(d, r).wait_send()


TILES = 4


def finish(dq, dk, dv, kg, wg, wk, wv, dq_out, dk_out, dv_out, ig_out, a, b, c, dq_in, dk_in, dv_in, into, out, through):
    handed = ((dq, dq_in, dq_out), (dk, dk_in, dk_out), (dv, dv_in, dv_out))
    inward = [pltpu.make_async_copy(src, via, through.at[i]) for i, (src, via, _) in enumerate(handed)]
    onward = [pltpu.make_async_copy(via, dst, through.at[3 + i]) for i, (_, via, dst) in enumerate(handed)]
    first = pltpu.make_async_copy(kg, a, into.at[TILES, 0])
    first.start()
    cols = b.shape[2] // TILES
    head = lax.axis_index("head")
    loads = []
    for n in range(TILES):
        r = pl.ds(n * cols, cols)
        own = pl.ds(pl.multiple_of(head * b.shape[2] + n * cols, cols), cols)
        part = [pltpu.make_async_copy(w.at[own], b.at[i, head, r], into.at[n, i]) for i, w in enumerate((wk, wv))]
        for i in range(2):
            for j in range(1, 4):
                h = (head + j) % 4
                part.append(pltpu.make_async_copy(wg.at[i, h, r], b.at[i, h, r], into.at[n, 2 + 3 * i + j - 1]))
        loads.append(part)
    for one in sum(loads, []) + inward:
        one.start()
    first.wait()
    stores = []
    for n in range(TILES):
        for one in loads[n]:
            one.wait()
        r = pl.ds(n * cols, cols)
        acc = None
        for w in range(2):
            for h in (0, 2):
                left = jnp.concatenate([a[w, h], a[w, h + 1]], axis=1)
                right = jnp.concatenate([b[w, h, r, :], b[w, h + 1, r, :]], axis=1)
                term = dot(left, right, NT)
                acc = term if acc is None else acc + term
        c[:, r] = acc.astype(BF16)
        stores.append(pltpu.make_async_copy(c.at[:, r], ig_out.at[:, r], out.at[n]))
        stores[-1].start()
        if n < 3:
            inward[n].wait()
            onward[n].start()
    for one in stores + onward:
        one.wait()


def _scratch():
    v, dma, smem = pltpu.VMEM, pltpu.SemaphoreType.DMA, pltpu.SMEM
    out = []
    for i in range(4):
        out += [(f"qs{i}", v((2, PIECE, 128), BF16)), (f"ds{i}", v((2, PIECE, 128), BF16))]
        out += [(f"qt{i}", v((2, 128, PIECE), BF16)), (f"dt{i}", v((2, 128, PIECE), BF16))]
        out += [(f"nrm{i}", v((2, PIECE, 128), F32)), (f"dlt{i}", v((2, PIECE, 128), F32))]
        out += [(f"dqa{i}", v((2, PIECE, 128), F32))]
    for i in range(2):
        out += [(f"nd{i}", v((16, 256), F32)), (f"dqs{i}", v((2, PIECE, 128), BF16))]
        out += [(f"dqr{i}", v((2, PIECE, 128), BF16))]
        for half in range(2):
            out += [(f"b{n}{i}{half}", v((ENTRIES + 3, 128, 128), F32)) for n in ("k", "v")]
            out += [(f"{n}b{half}", v((16, 128, 128), BF16)) for n in ("k", "v") if i == 0]
    out += [("tab", smem((16, 1, 128), I32)), ("tabz", smem((1, 1, 128), I32))]
    out += [("acck", v((16, 128, 128), F32)), ("accv", v((16, 128, 128), F32))]
    out += [("pos_lo", smem((32,), I32)), ("pos_hi", smem((32,), I32)), ("ent", smem((4 * ENTRIES,), I32))]
    out += [("vis", smem((4 * ENTRIES,), I32)), ("turn", smem((4,), I32))]
    out += [("sk", v((16, 128, 256), BF16)), ("sv", v((16, 128, 256), BF16))]
    for n in ("k", "v"):
        out += [(f"r1{n}", v((3, 4, 128, 256), BF16))]
        out += [(f"t2{n}", v((4, 128, 256), BF16)), (f"r2{n}", v((3, 128, 256), BF16))]
    out += [("fin", v((2, 256, 128), BF16))]
    out += [("k_send", dma((15,))), ("v_send", dma((15,))), ("k_recv", dma((16,))), ("v_recv", dma((16,)))]
    out += [("m_send", dma((7,))), ("m_recv", dma((16,))), ("m_row", dma((4,))), ("mz_recv", dma((1,)))]
    out += [("z_send", dma((7,))), ("z_recv", dma((7,))), ("w_send", dma((6,))), ("w_recv", dma((8,)))]
    out += [("fill", dma((2,))), ("s1k", dma((3,))), ("s1kr", dma((3,))), ("s1v", dma((12,))), ("s1vr", dma((12,)))]
    out += [("s2", dma((6,))), ("s2r", dma((6,)))]
    out += [("g_send", dma((6,))), ("g_recv", dma((8,)))]
    return out


SCRATCH = _scratch()


def per_device(
    query, key, value, attention_out, out_grad, log_norm, span_order, span_segment, key_weight, value_weight
):
    rows = query.shape[0]
    vmem, smem = pl.BlockSpec(memory_space=pltpu.VMEM), pl.BlockSpec(memory_space=pltpu.SMEM)
    hbm = pl.BlockSpec(memory_space=pl.ANY)
    columns = key_weight.shape[0] // 4
    small = (
        jax.ShapeDtypeStruct(query.shape, BF16),
        jax.ShapeDtypeStruct(key.shape, BF16),
        jax.ShapeDtypeStruct(value.shape, BF16),
    )
    held = pl.pallas_call(
        kernel,
        name="attention_backward",
        out_shape=small
        + (
            jax.ShapeDtypeStruct((2, 4, rows, HEAD_DIM), BF16),
            jax.ShapeDtypeStruct((2, 4, columns, HEAD_DIM), BF16),
        ),
        in_specs=[vmem] * 6 + [smem] * 2 + [hbm] * 2,
        out_specs=(vmem,) * 3 + (hbm,) * 2,
        scratch_shapes=[shape for _, shape in SCRATCH],
        compiler_params=pltpu.CompilerParams(
            collective_id=0, has_side_effects=True, vmem_limit_bytes=60 << 20
        ),
        cost_estimate=pl.CostEstimate(flops=11_000_000_000, bytes_accessed=16 << 20, transcendentals=0),
    )(
        query, out_grad, attention_out, log_norm.T, key, value,
        span_order, span_segment, key_weight, value_weight,
    )
    dma = pltpu.SemaphoreType.DMA
    return pl.pallas_call(
        finish,
        name="input_gradient",
        out_shape=small + (jax.ShapeDtypeStruct((rows, columns), BF16),),
        in_specs=[hbm] * 7,
        out_specs=(hbm,) * 4,
        scratch_shapes=[
            pltpu.VMEM((2, 4, rows, HEAD_DIM), BF16),
            pltpu.VMEM((2, 4, columns, HEAD_DIM), BF16),
            pltpu.VMEM((rows, columns), BF16),
            pltpu.VMEM(query.shape, BF16),
            pltpu.VMEM(key.shape, BF16),
            pltpu.VMEM(value.shape, BF16),
            dma((TILES + 1, 8)),
            dma((TILES,)),
            dma((6,)),
        ],
        compiler_params=pltpu.CompilerParams(vmem_limit_bytes=60 << 20),
        cost_estimate=pl.CostEstimate(flops=1_100_000_000, bytes_accessed=8 << 20, transcendentals=0),
    )(*held, key_weight, value_weight)


def solution(mesh):
    split = P("ctx", "head")
    in_specs = (split,) * 6 + (P("ctx"), P("ctx"), P(None, "head"), P(None, "head"))
    return jax.shard_map(
        per_device, mesh=mesh, in_specs=in_specs, out_specs=(split,) * 4, check_vma=False
    )
```

```python
import math

import jax
import jax.numpy as jnp
from jax import lax
from jax.experimental import pallas as pl
from jax.experimental.pallas import tpu as pltpu
from jax.sharding import PartitionSpec as P

HEAD_DIM = 128
SPAN = 128
GROUP = 8
SCALE = 1.0 / math.sqrt(HEAD_DIM)
LOG2E = math.log2(math.e)
HIDDEN = -1e30
MESH = pl.DeviceIdType.MESH
F32, BF16, I32 = jnp.float32, jnp.bfloat16, jnp.int32
NN = (((1,), (0,)), ((), ()))
NT = (((1,), (1,)), ((), ()))
PIECE = 4 * SPAN
STEPS = 3
ENTRIES = 4 * STEPS
EMPTY, DIAG_HI, DIAG_LO = ENTRIES, ENTRIES + 1, ENTRIES + 2
AROUND = (1, 3, 2)


def dot(a, b, dims=NN):
    return lax.dot_general(a, b, dims, preferred_element_type=F32)


def kernel(q, do, o, norm, k, v, order, segment, wk, wv, dq_out, dk_out, dv_out, kg, wg, *scratch):
    names = [n for n, _ in SCRATCH]
    s = dict(zip(names, scratch))
    qs, ds = [s[f"qs{i}"] for i in range(4)], [s[f"ds{i}"] for i in range(4)]
    qt, dt = [s[f"qt{i}"] for i in range(4)], [s[f"dt{i}"] for i in range(4)]
    nrm, dlt = [s[f"nrm{i}"] for i in range(4)], [s[f"dlt{i}"] for i in range(4)]
    dqa = [s[f"dqa{i}"] for i in range(4)]
    nd = [s["nd0"], s["nd1"]]
    tab, tabz = s["tab"], s["tabz"]
    kb, vb, acck, accv = [s["kb0"], s["kb1"]], [s["vb0"], s["vb1"]], s["acck"], s["accv"]
    bk = [[s[f"bk{g}{half}"] for half in range(2)] for g in range(2)]
    bv = [[s[f"bv{g}{half}"] for half in range(2)] for g in range(2)]
    pos_lo, pos_hi, ent, vis, turn = s["pos_lo"], s["pos_hi"], s["ent"], s["vis"], s["turn"]

    ctx, head = lax.axis_index("ctx"), lax.axis_index("head")
    z, y, x = ctx // 16, (ctx // 4) % 4, ctx % 4
    me = y * 4 + x

    def at_x(d):
        return (z * 16 + y * 4 + (x + d) % 4, head)

    def at_y(d):
        return (z * 16 + ((y + d) % 4) * 4 + x, head)

    over = ((1 - z) * 16 + me, head)
    mate = head + 1 - 2 * (head % 2)
    far, far_mate = (head + 2) % 4, 3 - head
    weight_peers = ((ctx, mate), ((1 - z) * 16 + me, far), ((1 - z) * 16 + me, far_mate))

    barrier = pltpu.get_barrier_semaphore()
    peers = [at_x(d) for d in AROUND] + [at_y(d) for d in AROUND] + [over]
    peers += [weight_peers[0], weight_peers[1], weight_peers[2], (ctx, far)]
    for peer in peers:
        pl.semaphore_signal(barrier, inc=1, device_id=peer, device_id_type=MESH)

    sent = []

    def copy(src, dst, send, recv, peer):
        return pltpu.make_async_remote_copy(
            src_ref=src, dst_ref=dst, send_sem=send, recv_sem=recv, device_id=peer, device_id_type=MESH
        )

    def push(src, dst, send, recv, peer):
        c = copy(src, dst, send, recv, peer)
        c.start()
        sent.append(c)

    def arrived(dst, send, recv):
        copy(dst, dst, send, recv, over).wait_recv()

    def swapped(sel, first, second):
        shape = first.shape
        turn_round = jnp.full(shape, order[0], I32) > jnp.full(shape, order[1], I32)
        return jnp.where(turn_round, second, first) if sel == 0 else jnp.where(turn_round, first, second)

    slots = (pl.ds(0, SPAN), pl.ds(SPAN, SPAN))

    for sel in range(2):
        kb[0][2 * x + sel] = swapped(sel, k[slots[0], :], k[slots[1], :])
        vb[0][2 * x + sel] = swapped(sel, v[slots[0], :], v[slots[1], :])
    for i, value in enumerate((order[0], order[1], segment[0], segment[1])):
        tab[me, 0, i] = value

    def stack(p):
        for sel in range(2):
            for hh in range(4):
                r = pl.ds(hh * SPAN, SPAN)
                c = pl.ds((p * 4 + hh) * HEAD_DIM, HEAD_DIM)
                qs[p][sel, r, :] = swapped(sel, q[slots[0], c], q[slots[1], c])
                ds[p][sel, r, :] = swapped(sel, do[slots[0], c], do[slots[1], c])

    stack(0)
    stack(1)
    pl.semaphore_wait(barrier, len(peers))

    ks, vs = s["k_send"], s["v_send"]
    kr, vr = s["k_recv"], s["v_recv"]
    ms, mr, mrow = s["m_send"], s["m_recv"], s["m_row"]

    def block(buf, r, u):
        return buf[r // 2].at[pl.ds(2 * (r % 2 * 4 + u), 2)]

    def along_x(buf, r, u, send, recv, d):
        push(block(buf, r, u), block(buf, r, u), send, recv.at[r * 4 + u], at_x(d))

    def along_y(buf, r, u, send, recv, d):
        there = (r + 4 - d) % 4
        push(block(buf, r, u), block(buf, there, u), send, recv.at[there * 4 + u], at_y(d))

    for i, d in enumerate(AROUND):
        push(tab.at[me], tab.at[me], ms.at[i], mr.at[me], at_x(d))
    for i, d in enumerate((1, 3)):
        along_x(kb, 0, x, ks.at[i], kr, d)
        along_y(vb, 0, x, vs.at[i], vr, d)
    along_x(kb, 0, x, ks.at[2], kr, 2)
    for i, d in enumerate(AROUND):
        along_x(vb, 0, x, vs.at[3 + i], vr, d)
    for i, d in enumerate((3, 1)):
        along_y(kb, 0, x, ks.at[3 + i], kr, d)
    zs, zr = s["z_send"], s["z_recv"]
    push(tab.at[me], tabz.at[0], ms.at[6], s["mz_recv"].at[0], over)
    push(qs[0], qs[2], zs.at[0], zr.at[0], over)
    push(ds[0], ds[2], zs.at[1], zr.at[1], over)
    ws, wr = s["w_send"], s["w_recv"]
    columns = wk.shape[0] // 4

    def weight_copy(i, w, j):
        peer = weight_peers[j]
        rows = pl.ds(pl.multiple_of(peer[1] * columns, columns), columns)
        return copy(w.at[rows], wg.at[i, head], ws.at[3 * i + j], wr.at[4 * i + head], peer)

    for i, w in enumerate((wk, wv)):
        for j in range(3):
            weight_copy(i, w, j).start()

    fill = []

    lane = lax.broadcasted_iota(I32, (2 * SPAN, 128), 1)
    sums = jnp.zeros((2 * SPAN, 128), F32)
    for h in range(GROUP):
        c = pl.ds(h * HEAD_DIM, HEAD_DIM)
        term = jnp.sum(do[:, c].astype(F32) * o[:, c].astype(F32), axis=1, keepdims=True)
        sums = jnp.where(lane == h, term, sums)
    sums = sums.T[0:8, :]
    for sel in range(2):
        c = pl.ds(sel * SPAN, SPAN)
        nd[0][0:8, c] = swapped(sel, norm[:, slots[0]], norm[:, slots[1]])
        nd[0][8:16, c] = swapped(sel, sums[:, :SPAN], sums[:, SPAN:])
    push(nd[0], nd[1], zs.at[2], zr.at[2], over)
    push(qs[1], qs[3], zs.at[3], zr.at[3], over)
    push(ds[1], ds[3], zs.at[4], zr.at[4], over)

    def spread(g):
        rows = jnp.concatenate([nd[g][...], jnp.zeros((112, 2 * SPAN), F32)], axis=0).T
        for p in range(2):
            for sel in range(2):
                part = rows[sel * SPAN : (sel + 1) * SPAN, :]
                for hh in range(4):
                    h, r = p * 4 + hh, pl.ds(hh * SPAN, SPAN)
                    nrm[2 * g + p][sel, r, :] = jnp.broadcast_to(part[:, h : h + 1] * LOG2E, (SPAN, 128))
                    dlt[2 * g + p][sel, r, :] = jnp.broadcast_to(part[:, 8 + h : 9 + h], (SPAN, 128))

    def turned(i):
        for sel in range(2):
            for hh in range(4):
                r = pl.ds(hh * SPAN, SPAN)
                qt[i][sel, :, r] = qs[i][sel, r, :].T
                dt[i][sel, :, r] = ds[i][sel, r, :].T

    def step(i, sel, k4, v4, bias=None, mask=None):
        n = k4.shape[0] // 128
        e = dot(qs[i][sel], k4, NT) * (SCALE * LOG2E) - jnp.concatenate([nrm[i][sel]] * n, axis=1)
        if bias is not None:
            e = e + bias
        if mask is not None:
            e = jnp.where(mask, e, HIDDEN)
        attend = jnp.exp2(e)
        grad = dot(ds[i][sel], v4, NT) - jnp.concatenate([dlt[i][sel]] * n, axis=1)
        score = (attend * grad).astype(BF16)
        return score, dot(qt[i][sel], score), dot(dt[i][sel], attend.astype(BF16))

    def bias_row(seen):
        return jnp.concatenate(
            [jnp.where(jnp.full((1, 128), one, I32) > 0, 0.0, HIDDEN) for one in seen], axis=1
        )

    def columns_of(a, u):
        return a[:, u * 128 : (u + 1) * 128]

    spread(0)
    turned(0)
    turned(1)
    for i, d in enumerate(AROUND):
        arrived(tab.at[y * 4 + (x + 4 - d) % 4], ms.at[0], mr.at[y * 4 + (x + 4 - d) % 4])
    for i, d in enumerate(AROUND):
        line = pl.ds(y * 4, 4)
        push(tab.at[line], tab.at[line], ms.at[3 + i], mrow.at[y], at_y(d))
    along_y(vb, 0, x, vs.at[2], vr, 2)
    for i, d in enumerate(AROUND):
        u = (x + 4 - d) % 4
        arrived(block(kb, 0, u), ks.at[0], kr.at[u])
        for n, e in enumerate((3, 1)):
            along_y(kb, 0, u, ks.at[6 + 3 * i + n], kr, e)
        if d != 2:
            r = (1, 3)[i]
            arrived(block(vb, r, x), vs.at[0], vr.at[4 * r + x])
            for n, e in enumerate(AROUND):
                along_x(vb, r, x, vs.at[6 + 3 * i + n], vr, e)

    def hand_on_last():
        along_y(kb, 0, x, ks.at[5], kr, 2)
        for i, d in enumerate(AROUND):
            along_y(kb, 0, (x + 4 - d) % 4, ks.at[8 + 3 * i], kr, 2)
        arrived(block(vb, 2, x), vs.at[0], vr.at[8 + x])
        for n, e in enumerate(AROUND):
            along_x(vb, 2, x, vs.at[12 + n], vr, e)

    row = lax.broadcasted_iota(I32, (PIECE, 128), 0) % SPAN
    below = lax.broadcasted_iota(I32, (PIECE, 128), 1) <= row
    for sel in range(2):
        k1, v1 = kb[0][2 * x + sel], vb[0][2 * x + sel]
        place = DIAG_HI if sel else DIAG_LO
        score, dk0, dv0 = step(0, sel, k1, v1, mask=below)
        dqa[0][sel] = dot(score, k1)
        score, dk1, dv1 = step(1, sel, k1, v1, mask=below)
        dqa[1][sel] = dot(score, k1)
        bk[0][0][place] = dk0 + dk1
        bv[0][0][place] = dv0 + dv1
    for b in (bk, bv):
        for g in range(2):
            for half in range(2):
                b[g][half][EMPTY] = jnp.zeros((128, 128), F32)
    for i in (2, 3):
        dqa[i][...] = jnp.zeros_like(dqa[i])

    def low_span(j):
        return jnp.minimum(tab[j, 0, 0], tab[j, 0, 1])

    def query_spans(t, j):
        first = t[j, 0, 0] < t[j, 0, 1]
        low = jnp.where(first, t[j, 0, 0], t[j, 0, 1])
        return low, jnp.where(first, t[j, 0, 2], t[j, 0, 3]), jnp.where(first, t[j, 0, 3], t[j, 0, 2])

    def device_at(half, n):
        return (y + 2 * half + n // 4) % 4 * 4 + n % 4

    def later_rows(pieces, half, line, seg_hi, fresh):
        k4 = jnp.concatenate([kb[half][8 * line + 2 * u] for u in range(4)], axis=0)
        v4 = jnp.concatenate([vb[half][8 * line + 2 * u] for u in range(4)], axis=0)
        bias = bias_row([low_span(device_at(half, 4 * line + u)) - seg_hi + 1 for u in range(4)])
        dks = dvs = None
        for i in pieces:
            score, dk, dv = step(i, 1, k4, v4, bias=bias)
            dqa[i][1] += dot(score, k4)
            dks, dvs = (dk, dv) if dks is None else (dks + dk, dvs + dv)
        for u in range(4):
            place = 8 * half + 4 * line + u
            if fresh:
                acck[place] = columns_of(dks, u)
                accv[place] = columns_of(dvs, u)
            else:
                acck[place] += columns_of(dks, u)
                accv[place] += columns_of(dvs, u)

    def sorted_rows(pieces, g, half, t):
        which = 2 * g + half
        sel = jnp.where(t >= turn[which], 1, 0)
        k4 = jnp.concatenate([kb[half][ent[which * ENTRIES + 4 * t + u]] for u in range(4)], axis=0)
        v4 = jnp.concatenate([vb[half][ent[which * ENTRIES + 4 * t + u]] for u in range(4)], axis=0)
        bias = bias_row([vis[which * ENTRIES + 4 * t + u] for u in range(4)])
        none = jnp.zeros_like(k4)
        early = jnp.full(k4.shape, sel, I32) == 0
        wide = jnp.concatenate([jnp.where(early, k4, none), jnp.where(early, none, k4)], axis=1)
        dks = dvs = None
        for i in pieces:
            score, dk, dv = step(i, sel, k4, v4, bias=bias)
            both = dot(score, wide)
            dqa[i][0] += both[:, :128]
            dqa[i][1] += both[:, 128:]
            dks, dvs = (dk, dv) if dks is None else (dks + dk, dvs + dv)
        for u in range(4):
            bk[g][half][4 * t + u] = columns_of(dks, u)
            bv[g][half][4 * t + u] = columns_of(dvs, u)

    lo_own, seg_lo_own, seg_hi_own = query_spans(tab, me)
    for r in range(1, 4):
        arrived(tab.at[pl.ds(((y + r) % 4) * 4, 4)], ms.at[0], mrow.at[(y + r) % 4])
    arrived(tabz.at[0], ms.at[0], s["mz_recv"].at[0])
    lo_over, seg_lo_over, seg_hi_over = query_spans(tabz, 0)
    for g, (low, seg_lo, seg_hi) in enumerate(
        ((lo_own, seg_lo_own, seg_hi_own), (lo_over, seg_lo_over, seg_hi_over))
    ):
        for half in range(2):
            which = 2 * g + half
            spans = [low_span(device_at(half, n)) for n in range(8)]
            before = sum(jnp.where(one < low, 1, 0) for one in spans)
            upto = sum(jnp.where(one <= low, 1, 0) for one in spans)
            first = (before + 3) // 4
            turn[which] = first

            def place(n, _, half=half, which=which, low=low, spans=spans, upto=upto, first=first):
                mine = low_span(device_at(half, n))
                rank = sum(jnp.where(one < mine, 1, 0) for one in spans)
                hi = 4 * first + rank - upto
                pos_lo[8 * which + n] = jnp.where(mine < low, rank, jnp.where(mine == low, DIAG_LO, EMPTY))
                pos_hi[8 * which + n] = jnp.where(mine > low, hi, jnp.where(mine == low, DIAG_HI, EMPTY))
                return 0

            lax.fori_loop(0, 8, place, 0)

            def entry(p, _, which=which, spans=spans, first=first, seg_lo=seg_lo, seg_hi=seg_hi):
                index, span = jnp.int32(0), jnp.int32(-1)
                for n in range(8):
                    is_lo, is_hi = pos_lo[8 * which + n] == p, pos_hi[8 * which + n] == p
                    index = jnp.where(is_lo, 2 * n, jnp.where(is_hi, 2 * n + 1, index))
                    span = jnp.where(is_lo, spans[n], jnp.where(is_hi, 63 - spans[n], span))
                seg = jnp.where(p < 4 * first, seg_lo, seg_hi)
                ent[which * ENTRIES + p] = index
                vis[which * ENTRIES + p] = jnp.where(span >= seg, 1, 0)
                return 0

            lax.fori_loop(0, ENTRIES, entry, 0)

    for half in range(2):

        def own_line(line, _, half=half):
            r = 2 * half + line
            for u in range(4):
                place = pl.ds(2 * (line * 4 + u), 2)

                if r > 0:
                    arrived(kb[half].at[place], ks.at[0], kr.at[4 * r + u])

                @pl.when(x != u)
                def _():
                    arrived(vb[half].at[place], vs.at[0], vr.at[4 * r + u])

            later_rows((0, 1), half, line, seg_hi_own, True)
            return 0

        if half == 0:
            own_line(0, 0)
            hand_on_last()
            own_line(1, 0)
        else:
            own_line(1, 0)
            own_line(0, 0)

        def own_sorted(t, _, half=half):
            sorted_rows((0, 1), 0, half, t)
            return 0

        lax.fori_loop(0, STEPS, own_sorted, 0, unroll=True)

    dqs, dqr = [s["dqs0"], s["dqs1"]], [s["dqr0"], s["dqr1"]]
    arrived(nd[1], zs.at[0], zr.at[2])
    spread(1)
    for p in range(2):
        arrived(qs[2 + p], zs.at[0], zr.at[3 * p])
        arrived(ds[2 + p], zs.at[0], zr.at[3 * p + 1])
        turned(2 + p)

    def total(acc, b, half, n):
        lo = acc[8 * half + n] + b[0][half][pos_lo[8 * half + n]] + b[1][half][pos_lo[16 + 8 * half + n]]
        hi = b[0][half][pos_hi[8 * half + n]] + b[1][half][pos_hi[16 + 8 * half + n]]
        return jnp.concatenate([lo, hi], axis=1).astype(BF16)

    sk, sv, r1k, r1v = s["sk"], s["sv"], s["r1k"], s["r1v"]
    s1k, s1v, s1kr, s1vr = s["s1k"], s["s1v"], s["s1kr"], s["s1vr"]

    def key_copy(d):
        return copy(sk.at[pl.ds(d * 4, 4)], r1k.at[d - 1], s1k.at[d - 1], s1kr.at[d - 1], at_y(d))

    def value_copy(d, r):
        n = (d - 1) * 4 + r
        return copy(sv.at[r * 4 + (x + d) % 4], r1v.at[d - 1, r], s1v.at[n], s1vr.at[n], at_x(d))

    for half in (1, 0):

        def over_sorted(t, _, half=half):
            sorted_rows((2, 3), 1, half, t)
            return 0

        lax.fori_loop(0, STEPS, over_sorted, 0, unroll=True)

        def over_line(i, _, half=half):
            line = i if half else 1 - i
            r = 2 * half + line
            later_rows((2, 3), half, line, seg_hi_over, False)
            for u in range(4):
                sk[r * 4 + u] = total(acck, bk, half, 4 * line + u)
                sv[r * 4 + u] = total(accv, bv, half, 4 * line + u)

            @pl.when(r > 0)
            def _():
                key_copy(r).start()

            for d in AROUND:
                value_copy(d, r).start()
            return 0

        lax.fori_loop(0, 2, over_line, 0)

    for p in range(2):
        dqs[p][...] = dqa[2 + p][...].astype(BF16)
        push(dqs[p], dqr[p], zs.at[5 + p], zr.at[5 + p], over)

    t2k, t2v, r2k, r2v = s["t2k"], s["t2v"], s["r2k"], s["r2v"]

    def value_back(d):
        return copy(t2v.at[d], r2v.at[d - 1], s["s2"].at[2 + d], s["s2r"].at[2 + d], at_y(d))

    def sum_values(r):
        for d in AROUND:
            value_copy(d, r).wait_recv()
        parts = sv[r * 4 + x].astype(F32) + r1v[0, r].astype(F32)
        t2v[r] = (parts + r1v[1, r].astype(F32) + r1v[2, r].astype(F32)).astype(BF16)
        if r:
            value_back(r).start()

    for r in (2, 3, 1):
        sum_values(r)
    for d in (1, 2, 3):
        key_copy(d).wait_recv()

    def sum_keys(u, _):
        parts = sk[u].astype(F32) + r1k[0, u].astype(F32)
        t2k[u] = (parts + r1k[1, u].astype(F32) + r1k[2, u].astype(F32)).astype(BF16)
        return 0

    lax.fori_loop(0, 4, sum_keys, 0)
    for i, d in enumerate(AROUND):
        push(t2k.at[(x + d) % 4], r2k.at[d - 1], s["s2"].at[i], s["s2r"].at[d - 1], at_x(d))
    sum_values(0)

    for p in range(2):
        arrived(dqr[p], zs.at[0], zr.at[5 + p])
        for hh in range(4):
            r, c = pl.ds(hh * SPAN, SPAN), pl.ds((p * 4 + hh) * HEAD_DIM, HEAD_DIM)
            both = [(dqa[p][sel, r, :] + dqr[p][sel, r, :].astype(F32)) * SCALE for sel in range(2)]
            for slot in range(2):
                dq_out[slots[slot], c] = swapped(slot, both[0], both[1]).astype(BF16)

    fin = s["fin"]
    for w, (t2, r2, mine, out, scale) in enumerate(
        ((t2k, r2k, x, dk_out, SCALE), (t2v, r2v, 0, dv_out, 1.0))
    ):
        for d in range(3):
            arrived(r2.at[d], s["s2"].at[0], s["s2r"].at[3 * w + d])
        whole = t2[mine].astype(F32) + r2[0].astype(F32) + r2[1].astype(F32) + r2[2].astype(F32)
        both = [(columns_of(whole, sel) * scale).T for sel in range(2)]
        for slot in range(2):
            low = swapped(slot, both[0], both[1]).astype(BF16)
            out[slots[slot], :] = low
            fin[w, slots[slot], :] = low
        fill.append(pltpu.make_async_copy(fin.at[w], kg.at[w, head], s["fill"].at[w]))
        fill[-1].start()
        for i, peer in enumerate(((ctx, far), (ctx, mate))):
            push(fin.at[w], kg.at[w, head], s["g_send"].at[3 * w + i], s["g_recv"].at[4 * w + head], peer)
    for w in range(2):
        arrived(kg.at[w, far], ws.at[0], s["g_recv"].at[4 * w + far])
        push(kg.at[w, far], kg.at[w, far], s["g_send"].at[3 * w + 2], s["g_recv"].at[4 * w + far], (ctx, mate))

    for w in range(2):
        for h in (mate, far_mate):
            arrived(kg.at[w, h], ws.at[0], s["g_recv"].at[4 * w + h])
        for j, h in enumerate((mate, far, far_mate)):
            arrived(wg.at[w, h], ws.at[0], wr.at[4 * w + h])
            weight_copy(w, (wk, wv)[w], j).wait_send()
    for c in fill:
        c.wait()
    for c in sent:
        c.wait_send()
    for d in (1, 2, 3):
        key_copy(d).wait_send()
        value_back(d).wait_send()
        for r in range(4):
            value_copy(d, r).wait_send()


TILES = 4


def finish(dq, dk, dv, kg, wg, wk, wv, dq_out, dk_out, dv_out, ig_out, a, b, c, dq_in, dk_in, dv_in, into, out, through):
    handed = ((dq, dq_in, dq_out), (dk, dk_in, dk_out), (dv, dv_in, dv_out))
    inward = [pltpu.make_async_copy(src, via, through.at[i]) for i, (src, via, _) in enumerate(handed)]
    onward = [pltpu.make_async_copy(via, dst, through.at[3 + i]) for i, (_, via, dst) in enumerate(handed)]
    first = pltpu.make_async_copy(kg, a, into.at[TILES, 0])
    first.start()
    cols = b.shape[2] // TILES
    head = lax.axis_index("head")
    loads = []
    for n in range(TILES):
        r = pl.ds(n * cols, cols)
        own = pl.ds(pl.multiple_of(head * b.shape[2] + n * cols, cols), cols)
        part = [pltpu.make_async_copy(w.at[own], b.at[i, head, r], into.at[n, i]) for i, w in enumerate((wk, wv))]
        for i in range(2):
            for j in range(1, 4):
                h = (head + j) % 4
                part.append(pltpu.make_async_copy(wg.at[i, h, r], b.at[i, h, r], into.at[n, 2 + 3 * i + j - 1]))
        loads.append(part)
    for one in sum(loads, []) + inward:
        one.start()
    first.wait()
    stores = []
    for n in range(TILES):
        for one in loads[n]:
            one.wait()
        r = pl.ds(n * cols, cols)
        acc = None
        for w in range(2):
            for h in (0, 2):
                left = jnp.concatenate([a[w, h], a[w, h + 1]], axis=1)
                right = jnp.concatenate([b[w, h, r, :], b[w, h + 1, r, :]], axis=1)
                term = dot(left, right, NT)
                acc = term if acc is None else acc + term
        c[:, r] = acc.astype(BF16)
        stores.append(pltpu.make_async_copy(c.at[:, r], ig_out.at[:, r], out.at[n]))
        stores[-1].start()
        if n < 3:
            inward[n].wait()
            onward[n].start()
    for one in stores + onward:
        one.wait()


def _scratch():
    v, dma, smem = pltpu.VMEM, pltpu.SemaphoreType.DMA, pltpu.SMEM
    out = []
    for i in range(4):
        out += [(f"qs{i}", v((2, PIECE, 128), BF16)), (f"ds{i}", v((2, PIECE, 128), BF16))]
        out += [(f"qt{i}", v((2, 128, PIECE), BF16)), (f"dt{i}", v((2, 128, PIECE), BF16))]
        out += [(f"nrm{i}", v((2, PIECE, 128), F32)), (f"dlt{i}", v((2, PIECE, 128), F32))]
        out += [(f"dqa{i}", v((2, PIECE, 128), F32))]
    for i in range(2):
        out += [(f"nd{i}", v((16, 256), F32)), (f"dqs{i}", v((2, PIECE, 128), BF16))]
        out += [(f"dqr{i}", v((2, PIECE, 128), BF16))]
        for half in range(2):
            out += [(f"b{n}{i}{half}", v((ENTRIES + 3, 128, 128), F32)) for n in ("k", "v")]
            out += [(f"{n}b{half}", v((16, 128, 128), BF16)) for n in ("k", "v") if i == 0]
    out += [("tab", smem((16, 1, 128), I32)), ("tabz", smem((1, 1, 128), I32))]
    out += [("acck", v((16, 128, 128), F32)), ("accv", v((16, 128, 128), F32))]
    out += [("pos_lo", smem((32,), I32)), ("pos_hi", smem((32,), I32)), ("ent", smem((4 * ENTRIES,), I32))]
    out += [("vis", smem((4 * ENTRIES,), I32)), ("turn", smem((4,), I32))]
    out += [("sk", v((16, 128, 256), BF16)), ("sv", v((16, 128, 256), BF16))]
    for n in ("k", "v"):
        out += [(f"r1{n}", v((3, 4, 128, 256), BF16))]
        out += [(f"t2{n}", v((4, 128, 256), BF16)), (f"r2{n}", v((3, 128, 256), BF16))]
    out += [("fin", v((2, 256, 128), BF16))]
    out += [("k_send", dma((15,))), ("v_send", dma((15,))), ("k_recv", dma((16,))), ("v_recv", dma((16,)))]
    out += [("m_send", dma((7,))), ("m_recv", dma((16,))), ("m_row", dma((4,))), ("mz_recv", dma((1,)))]
    out += [("z_send", dma((7,))), ("z_recv", dma((7,))), ("w_send", dma((6,))), ("w_recv", dma((8,)))]
    out += [("fill", dma((2,))), ("s1k", dma((3,))), ("s1kr", dma((3,))), ("s1v", dma((12,))), ("s1vr", dma((12,)))]
    out += [("s2", dma((6,))), ("s2r", dma((6,)))]
    out += [("g_send", dma((6,))), ("g_recv", dma((8,)))]
    return out


SCRATCH = _scratch()


def per_device(
    query, key, value, attention_out, out_grad, log_norm, span_order, span_segment, key_weight, value_weight
):
    rows = query.shape[0]
    vmem, smem = pl.BlockSpec(memory_space=pltpu.VMEM), pl.BlockSpec(memory_space=pltpu.SMEM)
    hbm = pl.BlockSpec(memory_space=pl.ANY)
    columns = key_weight.shape[0] // 4
    small = (
        jax.ShapeDtypeStruct(query.shape, BF16),
        jax.ShapeDtypeStruct(key.shape, BF16),
        jax.ShapeDtypeStruct(value.shape, BF16),
    )
    held = pl.pallas_call(
        kernel,
        name="attention_backward",
        out_shape=small
        + (
            jax.ShapeDtypeStruct((2, 4, rows, HEAD_DIM), BF16),
            jax.ShapeDtypeStruct((2, 4, columns, HEAD_DIM), BF16),
        ),
        in_specs=[vmem] * 6 + [smem] * 2 + [hbm] * 2,
        out_specs=(vmem,) * 3 + (hbm,) * 2,
        scratch_shapes=[shape for _, shape in SCRATCH],
        compiler_params=pltpu.CompilerParams(
            collective_id=0, has_side_effects=True, vmem_limit_bytes=60 << 20
        ),
        cost_estimate=pl.CostEstimate(flops=11_000_000_000, bytes_accessed=16 << 20, transcendentals=0),
    )(
        query, out_grad, attention_out, log_norm.T, key, value,
        span_order, span_segment, key_weight, value_weight,
    )
    dma = pltpu.SemaphoreType.DMA
    return pl.pallas_call(
        finish,
        name="input_gradient",
        out_shape=small + (jax.ShapeDtypeStruct((rows, columns), BF16),),
        in_specs=[hbm] * 7,
        out_specs=(hbm,) * 4,
        scratch_shapes=[
            pltpu.VMEM((2, 4, rows, HEAD_DIM), BF16),
            pltpu.VMEM((2, 4, columns, HEAD_DIM), BF16),
            pltpu.VMEM((rows, columns), BF16),
            pltpu.VMEM(query.shape, BF16),
            pltpu.VMEM(key.shape, BF16),
            pltpu.VMEM(value.shape, BF16),
            dma((TILES + 1, 8)),
            dma((TILES,)),
            dma((6,)),
        ],
        compiler_params=pltpu.CompilerParams(vmem_limit_bytes=60 << 20),
        cost_estimate=pl.CostEstimate(flops=1_100_000_000, bytes_accessed=8 << 20, transcendentals=0),
    )(*held, key_weight, value_weight)


def solution(mesh):
    split = P("ctx", "head")
    in_specs = (split,) * 6 + (P("ctx"), P("ctx"), P(None, "head"), P(None, "head"))
    return jax.shard_map(
        per_device, mesh=mesh, in_specs=in_specs, out_specs=(split,) * 4, check_vma=False
    )
```

```python
import math

import jax
import jax.numpy as jnp
from jax import lax
from jax.experimental import pallas as pl
from jax.experimental.pallas import tpu as pltpu
from jax.sharding import PartitionSpec as P

HEAD_DIM = 128
SPAN = 128
GROUP = 8
SCALE = 1.0 / math.sqrt(HEAD_DIM)
LOG2E = math.log2(math.e)
HIDDEN = -1e30
MESH = pl.DeviceIdType.MESH
F32, BF16, I32 = jnp.float32, jnp.bfloat16, jnp.int32
NN = (((1,), (0,)), ((), ()))
NT = (((1,), (1,)), ((), ()))
PIECE = 4 * SPAN
STEPS = 3
ENTRIES = 4 * STEPS
EMPTY, DIAG_HI, DIAG_LO = ENTRIES, ENTRIES + 1, ENTRIES + 2
AROUND = (1, 3, 2)


def dot(a, b, dims=NN):
    return lax.dot_general(a, b, dims, preferred_element_type=F32)


def kernel(q, do, o, norm, k, v, order, segment, wk, wv, dq_out, dk_out, dv_out, kg, wg, *scratch):
    names = [n for n, _ in SCRATCH]
    s = dict(zip(names, scratch))
    qs, ds = [s[f"qs{i}"] for i in range(4)], [s[f"ds{i}"] for i in range(4)]
    qt, dt = [s[f"qt{i}"] for i in range(4)], [s[f"dt{i}"] for i in range(4)]
    nrm, dlt = [s[f"nrm{i}"] for i in range(4)], [s[f"dlt{i}"] for i in range(4)]
    dqa = [s[f"dqa{i}"] for i in range(4)]
    nd = [s["nd0"], s["nd1"]]
    tab, tabz = s["tab"], s["tabz"]
    kb, vb, acck, accv = [s["kb0"], s["kb1"]], [s["vb0"], s["vb1"]], s["acck"], s["accv"]
    bk = [[s[f"bk{g}{half}"] for half in range(2)] for g in range(2)]
    bv = [[s[f"bv{g}{half}"] for half in range(2)] for g in range(2)]
    pos_lo, pos_hi, ent, vis, turn = s["pos_lo"], s["pos_hi"], s["ent"], s["vis"], s["turn"]

    ctx, head = lax.axis_index("ctx"), lax.axis_index("head")
    z, y, x = ctx // 16, (ctx // 4) % 4, ctx % 4
    me = y * 4 + x

    def at_x(d):
        return (z * 16 + y * 4 + (x + d) % 4, head)

    def at_y(d):
        return (z * 16 + ((y + d) % 4) * 4 + x, head)

    over = ((1 - z) * 16 + me, head)
    mate = head + 1 - 2 * (head % 2)
    far, far_mate = (head + 2) % 4, 3 - head
    weight_peers = ((ctx, mate), ((1 - z) * 16 + me, far), ((1 - z) * 16 + me, far_mate))

    barrier = pltpu.get_barrier_semaphore()
    peers = [at_x(d) for d in AROUND] + [at_y(d) for d in AROUND] + [over]
    peers += [weight_peers[0], weight_peers[1], weight_peers[2], (ctx, far)]
    for peer in peers:
        pl.semaphore_signal(barrier, inc=1, device_id=peer, device_id_type=MESH)

    sent = []

    def copy(src, dst, send, recv, peer):
        return pltpu.make_async_remote_copy(
            src_ref=src, dst_ref=dst, send_sem=send, recv_sem=recv, device_id=peer, device_id_type=MESH
        )

    def push(src, dst, send, recv, peer):
        c = copy(src, dst, send, recv, peer)
        c.start()
        sent.append(c)

    def arrived(dst, send, recv):
        copy(dst, dst, send, recv, over).wait_recv()

    def swapped(sel, first, second):
        shape = first.shape
        turn_round = jnp.full(shape, order[0], I32) > jnp.full(shape, order[1], I32)
        return jnp.where(turn_round, second, first) if sel == 0 else jnp.where(turn_round, first, second)

    slots = (pl.ds(0, SPAN), pl.ds(SPAN, SPAN))

    for sel in range(2):
        kb[0][2 * x + sel] = swapped(sel, k[slots[0], :], k[slots[1], :])
        vb[0][2 * x + sel] = swapped(sel, v[slots[0], :], v[slots[1], :])
    for i, value in enumerate((order[0], order[1], segment[0], segment[1])):
        tab[me, 0, i] = value

    def stack(p):
        for sel in range(2):
            for hh in range(4):
                r = pl.ds(hh * SPAN, SPAN)
                c = pl.ds((p * 4 + hh) * HEAD_DIM, HEAD_DIM)
                qs[p][sel, r, :] = swapped(sel, q[slots[0], c], q[slots[1], c])
                ds[p][sel, r, :] = swapped(sel, do[slots[0], c], do[slots[1], c])

    stack(0)
    pl.semaphore_wait(barrier, len(peers))

    ks, vs = s["k_send"], s["v_send"]
    kr, vr = s["k_recv"], s["v_recv"]
    ms, mr, mrow = s["m_send"], s["m_recv"], s["m_row"]

    def block(buf, r, u):
        return buf[r // 2].at[pl.ds(2 * (r % 2 * 4 + u), 2)]

    def along_x(buf, r, u, send, recv, d):
        push(block(buf, r, u), block(buf, r, u), send, recv.at[r * 4 + u], at_x(d))

    def along_y(buf, r, u, send, recv, d):
        there = (r + 4 - d) % 4
        push(block(buf, r, u), block(buf, there, u), send, recv.at[there * 4 + u], at_y(d))

    for i, d in enumerate(AROUND):
        push(tab.at[me], tab.at[me], ms.at[i], mr.at[me], at_x(d))
    for i, d in enumerate((1, 3)):
        along_x(kb, 0, x, ks.at[i], kr, d)
        along_y(vb, 0, x, vs.at[i], vr, d)
    along_x(kb, 0, x, ks.at[2], kr, 2)
    for i, d in enumerate(AROUND):
        along_x(vb, 0, x, vs.at[3 + i], vr, d)
    for i, d in enumerate((3, 1)):
        along_y(kb, 0, x, ks.at[3 + i], kr, d)
    zs, zr = s["z_send"], s["z_recv"]
    push(tab.at[me], tabz.at[0], ms.at[6], s["mz_recv"].at[0], over)
    push(qs[0], qs[2], zs.at[0], zr.at[0], over)
    push(ds[0], ds[2], zs.at[1], zr.at[1], over)
    ws, wr = s["w_send"], s["w_recv"]
    columns = wk.shape[0] // 4

    def weight_copy(i, w, j):
        peer = weight_peers[j]
        rows = pl.ds(pl.multiple_of(peer[1] * columns, columns), columns)
        return copy(w.at[rows], wg.at[i, head], ws.at[3 * i + j], wr.at[4 * i + head], peer)

    for i, w in enumerate((wk, wv)):
        for j in range(3):
            weight_copy(i, w, j).start()

    fill = []

    stack(1)
    lane = lax.broadcasted_iota(I32, (2 * SPAN, 128), 1)
    sums = jnp.zeros((2 * SPAN, 128), F32)
    for h in range(GROUP):
        c = pl.ds(h * HEAD_DIM, HEAD_DIM)
        term = jnp.sum(do[:, c].astype(F32) * o[:, c].astype(F32), axis=1, keepdims=True)
        sums = jnp.where(lane == h, term, sums)
    sums = sums.T[0:8, :]
    for sel in range(2):
        c = pl.ds(sel * SPAN, SPAN)
        nd[0][0:8, c] = swapped(sel, norm[:, slots[0]], norm[:, slots[1]])
        nd[0][8:16, c] = swapped(sel, sums[:, :SPAN], sums[:, SPAN:])
    push(nd[0], nd[1], zs.at[2], zr.at[2], over)
    push(qs[1], qs[3], zs.at[3], zr.at[3], over)
    push(ds[1], ds[3], zs.at[4], zr.at[4], over)

    def spread(g):
        rows = jnp.concatenate([nd[g][...], jnp.zeros((112, 2 * SPAN), F32)], axis=0).T
        for p in range(2):
            for sel in range(2):
                part = rows[sel * SPAN : (sel + 1) * SPAN, :]
                for hh in range(4):
                    h, r = p * 4 + hh, pl.ds(hh * SPAN, SPAN)
                    nrm[2 * g + p][sel, r, :] = jnp.broadcast_to(part[:, h : h + 1] * LOG2E, (SPAN, 128))
                    dlt[2 * g + p][sel, r, :] = jnp.broadcast_to(part[:, 8 + h : 9 + h], (SPAN, 128))

    def turned(i):
        for sel in range(2):
            for hh in range(4):
                r = pl.ds(hh * SPAN, SPAN)
                qt[i][sel, :, r] = qs[i][sel, r, :].T
                dt[i][sel, :, r] = ds[i][sel, r, :].T

    def step(i, sel, k4, v4, bias=None, mask=None):
        n = k4.shape[0] // 128
        e = dot(qs[i][sel], k4, NT) * (SCALE * LOG2E) - jnp.concatenate([nrm[i][sel]] * n, axis=1)
        if bias is not None:
            e = e + bias
        if mask is not None:
            e = jnp.where(mask, e, HIDDEN)
        attend = jnp.exp2(e)
        grad = dot(ds[i][sel], v4, NT) - jnp.concatenate([dlt[i][sel]] * n, axis=1)
        score = (attend * grad).astype(BF16)
        return score, dot(qt[i][sel], score), dot(dt[i][sel], attend.astype(BF16))

    def bias_row(seen):
        return jnp.concatenate(
            [jnp.where(jnp.full((1, 128), one, I32) > 0, 0.0, HIDDEN) for one in seen], axis=1
        )

    def columns_of(a, u):
        return a[:, u * 128 : (u + 1) * 128]

    spread(0)
    turned(0)
    turned(1)
    for i, d in enumerate(AROUND):
        arrived(tab.at[y * 4 + (x + 4 - d) % 4], ms.at[0], mr.at[y * 4 + (x + 4 - d) % 4])
    for i, d in enumerate(AROUND):
        line = pl.ds(y * 4, 4)
        push(tab.at[line], tab.at[line], ms.at[3 + i], mrow.at[y], at_y(d))
    along_y(vb, 0, x, vs.at[2], vr, 2)
    for i, d in enumerate(AROUND):
        u = (x + 4 - d) % 4
        arrived(block(kb, 0, u), ks.at[0], kr.at[u])
        for n, e in enumerate((3, 1)):
            along_y(kb, 0, u, ks.at[6 + 3 * i + n], kr, e)
        if d != 2:
            r = (1, 3)[i]
            arrived(block(vb, r, x), vs.at[0], vr.at[4 * r + x])
            for n, e in enumerate(AROUND):
                along_x(vb, r, x, vs.at[6 + 3 * i + n], vr, e)

    def hand_on_last():
        along_y(kb, 0, x, ks.at[5], kr, 2)
        for i, d in enumerate(AROUND):
            along_y(kb, 0, (x + 4 - d) % 4, ks.at[8 + 3 * i], kr, 2)
        arrived(block(vb, 2, x), vs.at[0], vr.at[8 + x])
        for n, e in enumerate(AROUND):
            along_x(vb, 2, x, vs.at[12 + n], vr, e)

    row = lax.broadcasted_iota(I32, (PIECE, 128), 0) % SPAN
    below = lax.broadcasted_iota(I32, (PIECE, 128), 1) <= row
    for sel in range(2):
        k1, v1 = kb[0][2 * x + sel], vb[0][2 * x + sel]
        place = DIAG_HI if sel else DIAG_LO
        score, dk0, dv0 = step(0, sel, k1, v1, mask=below)
        dqa[0][sel] = dot(score, k1)
        score, dk1, dv1 = step(1, sel, k1, v1, mask=below)
        dqa[1][sel] = dot(score, k1)
        bk[0][0][place] = dk0 + dk1
        bv[0][0][place] = dv0 + dv1
    for b in (bk, bv):
        for g in range(2):
            for half in range(2):
                b[g][half][EMPTY] = jnp.zeros((128, 128), F32)
    for i in (2, 3):
        dqa[i][...] = jnp.zeros_like(dqa[i])

    def low_span(j):
        return jnp.minimum(tab[j, 0, 0], tab[j, 0, 1])

    def query_spans(t, j):
        first = t[j, 0, 0] < t[j, 0, 1]
        low = jnp.where(first, t[j, 0, 0], t[j, 0, 1])
        return low, jnp.where(first, t[j, 0, 2], t[j, 0, 3]), jnp.where(first, t[j, 0, 3], t[j, 0, 2])

    def device_at(half, n):
        return (y + 2 * half + n // 4) % 4 * 4 + n % 4

    def later_rows(pieces, half, line, seg_hi, fresh):
        k4 = jnp.concatenate([kb[half][8 * line + 2 * u] for u in range(4)], axis=0)
        v4 = jnp.concatenate([vb[half][8 * line + 2 * u] for u in range(4)], axis=0)
        bias = bias_row([low_span(device_at(half, 4 * line + u)) - seg_hi + 1 for u in range(4)])
        dks = dvs = None
        for i in pieces:
            score, dk, dv = step(i, 1, k4, v4, bias=bias)
            dqa[i][1] += dot(score, k4)
            dks, dvs = (dk, dv) if dks is None else (dks + dk, dvs + dv)
        for u in range(4):
            place = 8 * half + 4 * line + u
            if fresh:
                acck[place] = columns_of(dks, u)
                accv[place] = columns_of(dvs, u)
            else:
                acck[place] += columns_of(dks, u)
                accv[place] += columns_of(dvs, u)

    def sorted_rows(pieces, g, half, t):
        which = 2 * g + half
        sel = jnp.where(t >= turn[which], 1, 0)
        k4 = jnp.concatenate([kb[half][ent[which * ENTRIES + 4 * t + u]] for u in range(4)], axis=0)
        v4 = jnp.concatenate([vb[half][ent[which * ENTRIES + 4 * t + u]] for u in range(4)], axis=0)
        bias = bias_row([vis[which * ENTRIES + 4 * t + u] for u in range(4)])
        none = jnp.zeros_like(k4)
        early = jnp.full(k4.shape, sel, I32) == 0
        wide = jnp.concatenate([jnp.where(early, k4, none), jnp.where(early, none, k4)], axis=1)
        dks = dvs = None
        for i in pieces:
            score, dk, dv = step(i, sel, k4, v4, bias=bias)
            both = dot(score, wide)
            dqa[i][0] += both[:, :128]
            dqa[i][1] += both[:, 128:]
            dks, dvs = (dk, dv) if dks is None else (dks + dk, dvs + dv)
        for u in range(4):
            bk[g][half][4 * t + u] = columns_of(dks, u)
            bv[g][half][4 * t + u] = columns_of(dvs, u)

    lo_own, seg_lo_own, seg_hi_own = query_spans(tab, me)
    for r in range(1, 4):
        arrived(tab.at[pl.ds(((y + r) % 4) * 4, 4)], ms.at[0], mrow.at[(y + r) % 4])
    arrived(tabz.at[0], ms.at[0], s["mz_recv"].at[0])
    lo_over, seg_lo_over, seg_hi_over = query_spans(tabz, 0)
    for g, (low, seg_lo, seg_hi) in enumerate(
        ((lo_own, seg_lo_own, seg_hi_own), (lo_over, seg_lo_over, seg_hi_over))
    ):
        for half in range(2):
            which = 2 * g + half
            spans = [low_span(device_at(half, n)) for n in range(8)]
            before = sum(jnp.where(one < low, 1, 0) for one in spans)
            upto = sum(jnp.where(one <= low, 1, 0) for one in spans)
            first = (before + 3) // 4
            turn[which] = first

            def place(n, _, half=half, which=which, low=low, spans=spans, upto=upto, first=first):
                mine = low_span(device_at(half, n))
                rank = sum(jnp.where(one < mine, 1, 0) for one in spans)
                hi = 4 * first + rank - upto
                pos_lo[8 * which + n] = jnp.where(mine < low, rank, jnp.where(mine == low, DIAG_LO, EMPTY))
                pos_hi[8 * which + n] = jnp.where(mine > low, hi, jnp.where(mine == low, DIAG_HI, EMPTY))
                return 0

            lax.fori_loop(0, 8, place, 0)

            def entry(p, _, which=which, spans=spans, first=first, seg_lo=seg_lo, seg_hi=seg_hi):
                index, span = jnp.int32(0), jnp.int32(-1)
                for n in range(8):
                    is_lo, is_hi = pos_lo[8 * which + n] == p, pos_hi[8 * which + n] == p
                    index = jnp.where(is_lo, 2 * n, jnp.where(is_hi, 2 * n + 1, index))
                    span = jnp.where(is_lo, spans[n], jnp.where(is_hi, 63 - spans[n], span))
                seg = jnp.where(p < 4 * first, seg_lo, seg_hi)
                ent[which * ENTRIES + p] = index
                vis[which * ENTRIES + p] = jnp.where(span >= seg, 1, 0)
                return 0

            lax.fori_loop(0, ENTRIES, entry, 0)

    for half in range(2):

        def own_line(line, _, half=half):
            r = 2 * half + line
            for u in range(4):
                place = pl.ds(2 * (line * 4 + u), 2)

                if r > 0:
                    arrived(kb[half].at[place], ks.at[0], kr.at[4 * r + u])

                @pl.when(x != u)
                def _():
                    arrived(vb[half].at[place], vs.at[0], vr.at[4 * r + u])

            later_rows((0, 1), half, line, seg_hi_own, True)
            return 0

        if half == 0:
            own_line(0, 0)
            hand_on_last()
            own_line(1, 0)
        else:
            own_line(1, 0)
            own_line(0, 0)

        def own_sorted(t, _, half=half):
            sorted_rows((0, 1), 0, half, t)
            return 0

        lax.fori_loop(0, STEPS, own_sorted, 0, unroll=True)

    dqs, dqr = [s["dqs0"], s["dqs1"]], [s["dqr0"], s["dqr1"]]
    arrived(nd[1], zs.at[0], zr.at[2])
    spread(1)
    for p in range(2):
        arrived(qs[2 + p], zs.at[0], zr.at[3 * p])
        arrived(ds[2 + p], zs.at[0], zr.at[3 * p + 1])
        turned(2 + p)

    def total(acc, b, half, n):
        lo = acc[8 * half + n] + b[0][half][pos_lo[8 * half + n]] + b[1][half][pos_lo[16 + 8 * half + n]]
        hi = b[0][half][pos_hi[8 * half + n]] + b[1][half][pos_hi[16 + 8 * half + n]]
        return jnp.concatenate([lo, hi], axis=1).astype(BF16)

    sk, sv, r1k, r1v = s["sk"], s["sv"], s["r1k"], s["r1v"]
    s1k, s1v, s1kr, s1vr = s["s1k"], s["s1v"], s["s1kr"], s["s1vr"]

    def key_copy(d):
        return copy(sk.at[pl.ds(d * 4, 4)], r1k.at[d - 1], s1k.at[d - 1], s1kr.at[d - 1], at_y(d))

    def value_copy(d, r):
        n = (d - 1) * 4 + r
        return copy(sv.at[r * 4 + (x + d) % 4], r1v.at[d - 1, r], s1v.at[n], s1vr.at[n], at_x(d))

    for half in (1, 0):

        def over_sorted(t, _, half=half):
            sorted_rows((2, 3), 1, half, t)
            return 0

        lax.fori_loop(0, STEPS, over_sorted, 0, unroll=True)

        def over_line(i, _, half=half):
            line = i if half else 1 - i
            r = 2 * half + line
            later_rows((2, 3), half, line, seg_hi_over, False)
            for u in range(4):
                sk[r * 4 + u] = total(acck, bk, half, 4 * line + u)
                sv[r * 4 + u] = total(accv, bv, half, 4 * line + u)

            @pl.when(r > 0)
            def _():
                key_copy(r).start()

            for d in AROUND:
                value_copy(d, r).start()
            return 0

        lax.fori_loop(0, 2, over_line, 0)

    for p in range(2):
        dqs[p][...] = dqa[2 + p][...].astype(BF16)
        push(dqs[p], dqr[p], zs.at[5 + p], zr.at[5 + p], over)

    t2k, t2v, r2k, r2v = s["t2k"], s["t2v"], s["r2k"], s["r2v"]

    def value_back(d):
        return copy(t2v.at[d], r2v.at[d - 1], s["s2"].at[2 + d], s["s2r"].at[2 + d], at_y(d))

    def sum_values(r):
        for d in AROUND:
            value_copy(d, r).wait_recv()
        parts = sv[r * 4 + x].astype(F32) + r1v[0, r].astype(F32)
        t2v[r] = (parts + r1v[1, r].astype(F32) + r1v[2, r].astype(F32)).astype(BF16)
        if r:
            value_back(r).start()

    for r in (2, 3, 1):
        sum_values(r)
    for d in (1, 2, 3):
        key_copy(d).wait_recv()

    def sum_keys(u, _):
        parts = sk[u].astype(F32) + r1k[0, u].astype(F32)
        t2k[u] = (parts + r1k[1, u].astype(F32) + r1k[2, u].astype(F32)).astype(BF16)
        return 0

    lax.fori_loop(0, 4, sum_keys, 0)
    for i, d in enumerate(AROUND):
        push(t2k.at[(x + d) % 4], r2k.at[d - 1], s["s2"].at[i], s["s2r"].at[d - 1], at_x(d))
    sum_values(0)

    fin = s["fin"]
    for w, (t2, r2, mine, out, scale) in enumerate(
        ((t2k, r2k, x, dk_out, SCALE), (t2v, r2v, 0, dv_out, 1.0))
    ):
        for d in range(3):
            arrived(r2.at[d], s["s2"].at[0], s["s2r"].at[3 * w + d])
        whole = t2[mine].astype(F32) + r2[0].astype(F32) + r2[1].astype(F32) + r2[2].astype(F32)
        both = [(columns_of(whole, sel) * scale).T for sel in range(2)]
        for slot in range(2):
            low = swapped(slot, both[0], both[1]).astype(BF16)
            out[slots[slot], :] = low
            fin[w, slots[slot], :] = low
        fill.append(pltpu.make_async_copy(fin.at[w], kg.at[w, head], s["fill"].at[w]))
        fill[-1].start()
        for i, peer in enumerate(((ctx, far), (ctx, mate))):
            push(fin.at[w], kg.at[w, head], s["g_send"].at[3 * w + i], s["g_recv"].at[4 * w + head], peer)
    for p in range(2):
        arrived(dqr[p], zs.at[0], zr.at[5 + p])
        for hh in range(4):
            r, c = pl.ds(hh * SPAN, SPAN), pl.ds((p * 4 + hh) * HEAD_DIM, HEAD_DIM)
            both = [(dqa[p][sel, r, :] + dqr[p][sel, r, :].astype(F32)) * SCALE for sel in range(2)]
            for slot in range(2):
                dq_out[slots[slot], c] = swapped(slot, both[0], both[1]).astype(BF16)

    for w in range(2):
        arrived(kg.at[w, far], ws.at[0], s["g_recv"].at[4 * w + far])
        push(kg.at[w, far], kg.at[w, far], s["g_send"].at[3 * w + 2], s["g_recv"].at[4 * w + far], (ctx, mate))

    for w in range(2):
        for h in (mate, far_mate):
            arrived(kg.at[w, h], ws.at[0], s["g_recv"].at[4 * w + h])
        for j, h in enumerate((mate, far, far_mate)):
            arrived(wg.at[w, h], ws.at[0], wr.at[4 * w + h])
            weight_copy(w, (wk, wv)[w], j).wait_send()
    for c in fill:
        c.wait()
    for c in sent:
        c.wait_send()
    for d in (1, 2, 3):
        key_copy(d).wait_send()
        value_back(d).wait_send()
        for r in range(4):
            value_copy(d, r).wait_send()


TILES = 4


def finish(dq, dk, dv, kg, wg, wk, wv, dq_out, dk_out, dv_out, ig_out, a, b, c, dq_in, dk_in, dv_in, into, out, through):
    handed = ((dq, dq_in, dq_out), (dk, dk_in, dk_out), (dv, dv_in, dv_out))
    inward = [pltpu.make_async_copy(src, via, through.at[i]) for i, (src, via, _) in enumerate(handed)]
    onward = [pltpu.make_async_copy(via, dst, through.at[3 + i]) for i, (_, via, dst) in enumerate(handed)]
    first = pltpu.make_async_copy(kg, a, into.at[TILES, 0])
    first.start()
    cols = b.shape[2] // TILES
    head = lax.axis_index("head")
    loads = []
    for n in range(TILES):
        r = pl.ds(n * cols, cols)
        own = pl.ds(pl.multiple_of(head * b.shape[2] + n * cols, cols), cols)
        part = [pltpu.make_async_copy(w.at[own], b.at[i, head, r], into.at[n, i]) for i, w in enumerate((wk, wv))]
        for i in range(2):
            for j in range(1, 4):
                h = (head + j) % 4
                part.append(pltpu.make_async_copy(wg.at[i, h, r], b.at[i, h, r], into.at[n, 2 + 3 * i + j - 1]))
        loads.append(part)
    for one in sum(loads, []) + inward:
        one.start()
    first.wait()
    stores = []
    for n in range(TILES):
        for one in loads[n]:
            one.wait()
        r = pl.ds(n * cols, cols)
        acc = None
        for w in range(2):
            for h in (0, 2):
                left = jnp.concatenate([a[w, h], a[w, h + 1]], axis=1)
                right = jnp.concatenate([b[w, h, r, :], b[w, h + 1, r, :]], axis=1)
                term = dot(left, right, NT)
                acc = term if acc is None else acc + term
        c[:, r] = acc.astype(BF16)
        stores.append(pltpu.make_async_copy(c.at[:, r], ig_out.at[:, r], out.at[n]))
        stores[-1].start()
        if n < 3:
            inward[n].wait()
            onward[n].start()
    for one in stores + onward:
        one.wait()


def _scratch():
    v, dma, smem = pltpu.VMEM, pltpu.SemaphoreType.DMA, pltpu.SMEM
    out = []
    for i in range(4):
        out += [(f"qs{i}", v((2, PIECE, 128), BF16)), (f"ds{i}", v((2, PIECE, 128), BF16))]
        out += [(f"qt{i}", v((2, 128, PIECE), BF16)), (f"dt{i}", v((2, 128, PIECE), BF16))]
        out += [(f"nrm{i}", v((2, PIECE, 128), F32)), (f"dlt{i}", v((2, PIECE, 128), F32))]
        out += [(f"dqa{i}", v((2, PIECE, 128), F32))]
    for i in range(2):
        out += [(f"nd{i}", v((16, 256), F32)), (f"dqs{i}", v((2, PIECE, 128), BF16))]
        out += [(f"dqr{i}", v((2, PIECE, 128), BF16))]
        for half in range(2):
            out += [(f"b{n}{i}{half}", v((ENTRIES + 3, 128, 128), F32)) for n in ("k", "v")]
            out += [(f"{n}b{half}", v((16, 128, 128), BF16)) for n in ("k", "v") if i == 0]
    out += [("tab", smem((16, 1, 128), I32)), ("tabz", smem((1, 1, 128), I32))]
    out += [("acck", v((16, 128, 128), F32)), ("accv", v((16, 128, 128), F32))]
    out += [("pos_lo", smem((32,), I32)), ("pos_hi", smem((32,), I32)), ("ent", smem((4 * ENTRIES,), I32))]
    out += [("vis", smem((4 * ENTRIES,), I32)), ("turn", smem((4,), I32))]
    out += [("sk", v((16, 128, 256), BF16)), ("sv", v((16, 128, 256), BF16))]
    for n in ("k", "v"):
        out += [(f"r1{n}", v((3, 4, 128, 256), BF16))]
        out += [(f"t2{n}", v((4, 128, 256), BF16)), (f"r2{n}", v((3, 128, 256), BF16))]
    out += [("fin", v((2, 256, 128), BF16))]
    out += [("k_send", dma((15,))), ("v_send", dma((15,))), ("k_recv", dma((16,))), ("v_recv", dma((16,)))]
    out += [("m_send", dma((7,))), ("m_recv", dma((16,))), ("m_row", dma((4,))), ("mz_recv", dma((1,)))]
    out += [("z_send", dma((7,))), ("z_recv", dma((7,))), ("w_send", dma((6,))), ("w_recv", dma((8,)))]
    out += [("fill", dma((2,))), ("s1k", dma((3,))), ("s1kr", dma((3,))), ("s1v", dma((12,))), ("s1vr", dma((12,)))]
    out += [("s2", dma((6,))), ("s2r", dma((6,)))]
    out += [("g_send", dma((6,))), ("g_recv", dma((8,)))]
    return out


SCRATCH = _scratch()


def per_device(
    query, key, value, attention_out, out_grad, log_norm, span_order, span_segment, key_weight, value_weight
):
    rows = query.shape[0]
    vmem, smem = pl.BlockSpec(memory_space=pltpu.VMEM), pl.BlockSpec(memory_space=pltpu.SMEM)
    hbm = pl.BlockSpec(memory_space=pl.ANY)
    columns = key_weight.shape[0] // 4
    small = (
        jax.ShapeDtypeStruct(query.shape, BF16),
        jax.ShapeDtypeStruct(key.shape, BF16),
        jax.ShapeDtypeStruct(value.shape, BF16),
    )
    held = pl.pallas_call(
        kernel,
        name="attention_backward",
        out_shape=small
        + (
            jax.ShapeDtypeStruct((2, 4, rows, HEAD_DIM), BF16),
            jax.ShapeDtypeStruct((2, 4, columns, HEAD_DIM), BF16),
        ),
        in_specs=[vmem] * 6 + [smem] * 2 + [hbm] * 2,
        out_specs=(vmem,) * 3 + (hbm,) * 2,
        scratch_shapes=[shape for _, shape in SCRATCH],
        compiler_params=pltpu.CompilerParams(
            collective_id=0, has_side_effects=True, vmem_limit_bytes=60 << 20
        ),
        cost_estimate=pl.CostEstimate(flops=11_000_000_000, bytes_accessed=16 << 20, transcendentals=0),
    )(
        query, out_grad, attention_out, log_norm.T, key, value,
        span_order, span_segment, key_weight, value_weight,
    )
    dma = pltpu.SemaphoreType.DMA
    return pl.pallas_call(
        finish,
        name="input_gradient",
        out_shape=small + (jax.ShapeDtypeStruct((rows, columns), BF16),),
        in_specs=[hbm] * 7,
        out_specs=(hbm,) * 4,
        scratch_shapes=[
            pltpu.VMEM((2, 4, rows, HEAD_DIM), BF16),
            pltpu.VMEM((2, 4, columns, HEAD_DIM), BF16),
            pltpu.VMEM((rows, columns), BF16),
            pltpu.VMEM(query.shape, BF16),
            pltpu.VMEM(key.shape, BF16),
            pltpu.VMEM(value.shape, BF16),
            dma((TILES + 1, 8)),
            dma((TILES,)),
            dma((6,)),
        ],
        compiler_params=pltpu.CompilerParams(vmem_limit_bytes=60 << 20),
        cost_estimate=pl.CostEstimate(flops=1_100_000_000, bytes_accessed=8 << 20, transcendentals=0),
    )(*held, key_weight, value_weight)


def solution(mesh):
    split = P("ctx", "head")
    in_specs = (split,) * 6 + (P("ctx"), P("ctx"), P(None, "head"), P(None, "head"))
    return jax.shard_map(
        per_device, mesh=mesh, in_specs=in_specs, out_specs=(split,) * 4, check_vma=False
    )
```
